128 devices in a mesh: grp: 4 (over y_hi, core), chan: 16 (over z, x), tile: 2 (over y_lo).
Axes of the slice: x: 4, y: 4 (y_hi: 2, y_lo: 2; y = y_hi * 2 + y_lo), z: 4, core: 2. Of those that a mesh axis runs over, the one named last changes fastest.
Arguments:
- voltages: bfloat16 [1024, 512, 2, 1024], P(('grp', 'tile'), 'chan'), may hold values from -6 to 6
- taps: float32 [8, 1024], replicated, may hold values from -0.0625 to 0.0625
Outputs:
- vis_real: float32 [256, 36, 128, 128], P(('grp', 'chan', 'tile'))
- vis_imag: float32 [256, 36, 128, 128], P(('grp', 'chan', 'tile'))
The draws below stay inside these ranges and needn't reach their ends.
All inputs are finite; a program needn't handle non-finite values.
Results may differ from the reference program's by a relative error of at most 0.004.
Values may be sent and summed in bfloat16 or wider, within the bound.
No kernel may reach another device: no remote copies, remote signals or barrier semaphores. Data moves between devices by JAX's collectives and lax.ppermute only.
A program may use at most 256 MiB of HBM per device.

```python
import math
import jax
import jax.numpy as jnp
from jax import lax

ANTENNA_COUNT = 1024
FRAME_SAMPLES = 1024
FILTER_TAPS = 8
ANTENNA_BLOCKS = 8
SPECTRA_COUNT = 512
KEPT_CHANNELS = 256
TILE_ANTENNAS = 128


def level_of(rng, shape, cuts, least, largest):
    def one(position, shards_of):
        draws = jax.random.uniform(jax.random.fold_in(jax.random.fold_in(rng, 6), position), (shards_of,), jnp.float32, least / len(cuts), largest / len(cuts))
        return jnp.repeat(jnp.exp(draws), shape[position] // shards_of).reshape((-1,) + (1,) * (len(shape) - position - 1))

    level = one(*cuts[0])
    for cut in cuts[1:]:
        level = level * one(*cut)
    return level


def bell_draw(own_key, shape, spread, most, pieces=(), held_as=jnp.bfloat16):
    array = jax.random.normal(own_key, shape, jnp.float32) * spread
    if len(pieces) > 0:
        array = level_of(own_key, shape, pieces, -0.22, 0.18) * array
    return jnp.clip(array, min=-most, max=most).astype(held_as)


def setup_inputs(seed: int = 0) -> dict:
    keys = jax.random.split(jax.random.key(seed), 3)
    voltages = bell_draw(keys[0], (ANTENNA_COUNT, SPECTRA_COUNT, 2, FRAME_SAMPLES), 1.0, 6.0, ((0, 8), (1, 16)))
    taps = bell_draw(keys[1], (FILTER_TAPS, FRAME_SAMPLES), (FILTER_TAPS * FRAME_SAMPLES) ** -0.5, 0.0625, (), jnp.float32)
    return dict(voltages=voltages, taps=taps)


def transform_table(length, window):
    sample = jnp.arange(length, dtype=jnp.int32)[:, None]
    channel = jnp.arange(window, dtype=jnp.int32)[None, :]
    angles = ((sample * channel) % length).astype(jnp.float32) * (2.0 * math.pi / length)
    cosine = jnp.cos(angles)
    sine_part = jnp.sin(angles)
    upper_half = jnp.concatenate([cosine, -sine_part], axis=1)
    bottom = jnp.concatenate([sine_part, cosine], axis=1)
    return jnp.concatenate([upper_half, bottom], axis=0)


def split_into_channels(antenna_block, taps, fourier_transform):
    padded_samples = jnp.pad(antenna_block, ((0, 0), (FILTER_TAPS - 1, 0), (0, 0), (0, 0)))
    running_total = jnp.zeros(antenna_block.shape, jnp.float32)
    for tap_index in range(FILTER_TAPS):
        offset_frame = FILTER_TAPS - 1 - tap_index
        frames = padded_samples[:, offset_frame:offset_frame + SPECTRA_COUNT].astype(jnp.float32)
        running_total = running_total + taps[tap_index][None, None, None, :] * frames
    frame_matrix = running_total.reshape(-1, 2 * FRAME_SAMPLES)
    spectra_stack = jnp.dot(frame_matrix, fourier_transform, preferred_element_type=jnp.float32, precision=lax.Precision.HIGHEST).astype(jnp.bfloat16)
    return spectra_stack.reshape(antenna_block.shape[0], SPECTRA_COUNT, 2 * KEPT_CHANNELS)


def upper_tile_list(matrix):
    blocked = matrix.reshape(ANTENNA_BLOCKS, TILE_ANTENNAS, ANTENNA_BLOCKS, TILE_ANTENNAS).transpose(0, 2, 1, 3)
    return jnp.concatenate([blocked[row_block, row_block:] for row_block in range(ANTENNA_BLOCKS)], axis=0)


def correlate(channel_matrix):
    swapped = jnp.concatenate([channel_matrix[:, SPECTRA_COUNT:], -channel_matrix[:, :SPECTRA_COUNT]], axis=1)
    stacked_rows = jnp.concatenate([channel_matrix, swapped], axis=0)
    cross_products = jnp.dot(stacked_rows, channel_matrix.T, preferred_element_type=jnp.float32) * (1.0 / SPECTRA_COUNT)
    return upper_tile_list(cross_products[:ANTENNA_COUNT]), upper_tile_list(cross_products[ANTENNA_COUNT:])


def reference(voltages, taps):
    fourier_transform = transform_table(FRAME_SAMPLES, KEPT_CHANNELS)
    antenna_blocks = voltages.reshape(ANTENNA_BLOCKS, TILE_ANTENNAS, SPECTRA_COUNT, 2, FRAME_SAMPLES)
    spectra_stack = lax.map(lambda antenna_block: split_into_channels(antenna_block, taps, fourier_transform), antenna_blocks)
    spectra_stack = lax.optimization_barrier(spectra_stack.reshape(ANTENNA_COUNT, SPECTRA_COUNT, 2, KEPT_CHANNELS))
    channel_wise = spectra_stack.transpose(3, 0, 2, 1).reshape(KEPT_CHANNELS, ANTENNA_COUNT, 2 * SPECTRA_COUNT)
    vis_real, vis_imag = lax.map(correlate, channel_wise)
    return (vis_real, vis_imag)
```

```python
import functools

import jax
import jax.numpy as jnp
import ml_dtypes
import numpy as np
from jax import lax
from jax.experimental import pallas as pl
from jax.experimental.pallas import tpu as pltpu
from jax.sharding import PartitionSpec as P

ANTENNA_COUNT = 1024
FRAME_SAMPLES = 1024
FILTER_TAPS = 8
ANTENNA_BLOCKS = 8
SPECTRA_COUNT = 512
DEVICE_CHANNELS = 2
TILE_ANTENNAS = 128
DEVICES = 128
FRAMES = 32
CHUNK = 8
OUT_FRAMES = FRAMES + CHUNK
HALF = FRAME_SAMPLES // 2
AXES = ("grp", "chan", "tile")


def transform_tables():
    sample = np.arange(HALF)
    parts = []
    for odd in range(2):
        channel = 2 * np.arange(DEVICES) + odd
        angle = 2.0 * np.pi * ((sample[:, None] * channel[None, :]) % FRAME_SAMPLES) / FRAME_SAMPLES
        cosine, sine = np.cos(angle), np.sin(angle)
        from_real = np.concatenate([cosine, -sine], axis=1)
        from_imag = np.concatenate([sine, cosine], axis=1)
        both = np.stack([from_real.reshape(4, 128, 256), from_imag.reshape(4, 128, 256)], axis=1)
        parts.append(both.reshape(FRAME_SAMPLES, 256))
    table = np.stack(parts).astype(np.float32)
    high = table.astype(ml_dtypes.bfloat16)
    low = (table - high.astype(np.float32)).astype(ml_dtypes.bfloat16)
    return high, low


def filterbank_kernel(x_hbm, taps_ref, high_ref, low_ref, out_ref, x_v, plus, minus, spectra, sems):
    z_refs = (plus, minus)
    chunks = FRAMES // CHUNK
    copies = [
        pltpu.make_async_copy(
            x_hbm.at[:, pl.ds(CHUNK * i, CHUNK)], x_v.at[:, pl.ds(CHUNK * i, CHUNK)], sems.at[i]
        )
        for i in range(chunks)
    ]
    for copy in copies:
        copy.start()
    for i in range(chunks + 1):
        if i < chunks:
            copies[i].wait()

        def filter_antenna(a, _):
            frames = {
                s: x_v[a, s].astype(jnp.float32)
                for s in range(CHUNK * i - FILTER_TAPS + 1, CHUNK * (i + 1))
                if 0 <= s < FRAMES
            }
            rows = pl.ds(pl.multiple_of(a * 8, 8), 8)
            for q in range(CHUNK):
                total = jnp.zeros((16, 128), jnp.float32)
                for k in range(FILTER_TAPS):
                    s = CHUNK * i + q - k
                    if s in frames:
                        total = total + taps_ref[k] * frames[s]
                plus[q, rows, :] = total[:8] + total[8:]
                minus[q, rows, :] = total[:8] - total[8:]
            return 0

        lax.fori_loop(0, TILE_ANTENNAS, filter_antenna, 0, unroll=2)
        for odd in range(2):

            def transform(q, _):
                highs, lows = [], []
                for row in range(8):
                    z = jnp.concatenate(
                        [z_refs[odd][2 * q + e, pl.ds(row, TILE_ANTENNAS, stride=8), :] for e in range(2)],
                        axis=0,
                    )
                    high = z.astype(jnp.bfloat16)
                    highs.append(high)
                    lows.append((z - high.astype(jnp.float32)).astype(jnp.bfloat16))
                high = jnp.concatenate(highs, axis=1)
                low = jnp.concatenate(lows, axis=1)
                dot = functools.partial(jnp.dot, preferred_element_type=jnp.float32)
                found = (
                    dot(high, high_ref[odd]) + dot(low, high_ref[odd]) + dot(high, low_ref[odd])
                ).T
                for e in range(2):
                    spectra[odd, pl.ds(2 * q + e, 256, stride=CHUNK), :] = found[:, 128 * e : 128 * e + 128]
                return 0

            lax.fori_loop(0, CHUNK // 2, transform, 0)
            for part in range(2):
                rows = spectra[odd, 1024 * part : 1024 * part + 1024, :].reshape(DEVICES, CHUNK, 128)
                out_ref[:, odd, part, CHUNK * i : CHUNK * (i + 1), :] = rows.astype(jnp.bfloat16)


def filterbank(voltages, taps):
    frames = voltages.reshape(TILE_ANTENNAS, FRAMES, 2, 8, 128).transpose(0, 1, 3, 2, 4)
    frames = frames.reshape(TILE_ANTENNAS, FRAMES, 16, 128)
    taps_rows = jnp.broadcast_to(taps.reshape(8, 8, 1, 128), (8, 8, 2, 128)).reshape(8, 16, 128)
    high, low = transform_tables()
    vmem = pl.BlockSpec(memory_space=pltpu.VMEM)
    return pl.pallas_call(
        filterbank_kernel,
        out_shape=jax.ShapeDtypeStruct((DEVICES, 2, 2, OUT_FRAMES, 128), jnp.bfloat16),
        in_specs=[pl.BlockSpec(memory_space=pl.ANY), vmem, vmem, vmem],
        out_specs=vmem,
        scratch_shapes=[
            pltpu.VMEM((TILE_ANTENNAS, FRAMES, 16, 128), jnp.bfloat16),
            pltpu.VMEM((CHUNK, 1024, 128), jnp.float32),
            pltpu.VMEM((CHUNK, 1024, 128), jnp.float32),
            pltpu.VMEM((2, 256 * CHUNK, 128), jnp.float32),
            pltpu.SemaphoreType.DMA((4,)),
        ],
        compiler_params=pltpu.CompilerParams(vmem_limit_bytes=56 * 2**20),
    )(frames, taps_rows, jnp.asarray(high), jnp.asarray(low))


def correlate_kernel(in_ref, real_ref, imag_ref, y, yt):
    for b in range(ANTENNA_BLOCKS):
        grp, tile = b // 2, b % 2
        for part in range(2):

            def join(t, _):
                src = (grp * 16 + t) * 2 + tile
                before = jnp.maximum(src - 2, 0)
                tail = in_ref[before, 0, part, FRAMES:OUT_FRAMES, :].astype(jnp.float32)
                tail = jnp.where(t > 0, tail, 0.0)
                own = in_ref[src, 0, part, 0:FRAMES, :]
                head = (own[:CHUNK].astype(jnp.float32) + tail).astype(jnp.bfloat16)
                rows = pl.ds(pl.multiple_of(part * 512 + t * FRAMES, FRAMES), FRAMES)
                y[rows, 128 * b : 128 * b + 128] = jnp.concatenate([head, own[CHUNK:]], axis=0)
                return 0

            lax.fori_loop(0, 16, join, 0, unroll=4)
        yt[128 * b : 128 * b + 128, :] = y[:, 128 * b : 128 * b + 128].T
    dot = functools.partial(jnp.dot, preferred_element_type=jnp.float32)
    scale = 1.0 / SPECTRA_COUNT

    def first(i):
        return ANTENNA_BLOCKS * i - i * (i - 1) // 2

    for pair in range(ANTENNA_BLOCKS // 2):
        rows = yt[256 * pair : 256 * pair + 256, :]
        for other in range(pair, ANTENNA_BLOCKS // 2):
            columns = slice(256 * other, 256 * other + 256)
            real = dot(rows, y[:, columns]) * scale
            imag = (dot(rows[:, 512:], y[:512, columns]) - dot(rows[:, :512], y[512:, columns])) * scale
            for a in range(2):
                for b in range(2):
                    i, j = 2 * pair + a, 2 * other + b
                    if i <= j:
                        p = first(i) + j - i
                        real_ref[0, p] = real[128 * a : 128 * a + 128, 128 * b : 128 * b + 128]
                        imag_ref[0, p] = imag[128 * a : 128 * a + 128, 128 * b : 128 * b + 128]


def correlate(received):
    pairs = ANTENNA_BLOCKS * (ANTENNA_BLOCKS + 1) // 2
    out = jax.ShapeDtypeStruct((DEVICE_CHANNELS, pairs, 128, 128), jnp.float32)
    out_spec = pl.BlockSpec((1, pairs, 128, 128), lambda c: (c, 0, 0, 0))
    return pl.pallas_call(
        correlate_kernel,
        grid=(DEVICE_CHANNELS,),
        out_shape=(out, out),
        in_specs=[pl.BlockSpec((DEVICES, 1, 2, OUT_FRAMES, 128), lambda c: (0, c, 0, 0, 0))],
        out_specs=(out_spec, out_spec),
        scratch_shapes=[
            pltpu.VMEM((1024, ANTENNA_COUNT), jnp.bfloat16),
            pltpu.VMEM((ANTENNA_COUNT, 1024), jnp.bfloat16),
        ],
        compiler_params=pltpu.CompilerParams(vmem_limit_bytes=56 * 2**20),
    )(received)


def on_device(voltages, taps):
    departing = filterbank(voltages, taps)
    received = lax.all_to_all(departing, AXES, split_axis=0, concat_axis=0, tiled=True)
    return correlate(received)


def solution(mesh):
    in_specs = (P(("grp", "tile"), "chan", None, None), P())
    out_specs = (P(AXES, None, None, None), P(AXES, None, None, None))
    return jax.shard_map(
        on_device, mesh=mesh, in_specs=in_specs, out_specs=out_specs, check_vma=False
    )
```

```python
import functools

import jax
import jax.numpy as jnp
import ml_dtypes
import numpy as np
from jax import lax
from jax.experimental import pallas as pl
from jax.experimental.pallas import tpu as pltpu
from jax.sharding import PartitionSpec as P

ANTENNA_COUNT = 1024
FRAME_SAMPLES = 1024
FILTER_TAPS = 8
ANTENNA_BLOCKS = 8
SPECTRA_COUNT = 512
DEVICE_CHANNELS = 2
TILE_ANTENNAS = 128
DEVICES = 128
FRAMES = 32
UNIT = 8
PIECE = 4
TIME_BLOCKS = 16
PAIRS = ANTENNA_BLOCKS * (ANTENNA_BLOCKS + 1) // 2
HALF = FRAME_SAMPLES // 2
AXES = ("grp", "chan", "tile")

EARLY_UNITS = (0, 32, 8)
LATE_UNITS = (16, 24)
KEPT = 16
DEPTH = KEPT * TIME_BLOCKS


def transform_tables():
    sample = np.arange(HALF)
    parts = []
    for odd in range(2):
        channel = 2 * np.arange(DEVICES) + odd
        angle = 2.0 * np.pi * ((sample[:, None] * channel[None, :]) % FRAME_SAMPLES) / FRAME_SAMPLES
        cosine, sine = np.cos(angle), np.sin(angle)
        from_real = np.concatenate([cosine, -sine], axis=1)
        from_imag = np.concatenate([sine, cosine], axis=1)
        both = np.stack([from_real.reshape(4, 128, 256), from_imag.reshape(4, 128, 256)], axis=1)
        parts.append(both.reshape(FRAME_SAMPLES, 256))
    table = np.stack(parts).astype(np.float32)
    high = table.astype(ml_dtypes.bfloat16)
    low = (table - high.astype(np.float32)).astype(ml_dtypes.bfloat16)
    return high, low


def filterbank_kernel(units, order, x_hbm, taps_ref, high_hbm, low_hbm, out_hbm, *scratch):
    x_v, taps_rows, high_ref, low_ref, z, spectra, out_v, x_sems, table_sems, out_sems = scratch
    slot = {piece: i for i, piece in enumerate(order)}
    copies = [
        pltpu.make_async_copy(
            x_hbm.at[:, pl.ds(PIECE * piece, PIECE)], x_v.at[:, pl.ds(PIECE * i, PIECE)], x_sems.at[i]
        )
        for i, piece in enumerate(order)
    ]
    tables = [
        pltpu.make_async_copy(high_hbm, high_ref, table_sems.at[0]),
        pltpu.make_async_copy(low_hbm, low_ref, table_sems.at[1]),
    ]
    for copy in copies[:2] + tables + copies[2:]:
        copy.start()
    for k in range(FILTER_TAPS):
        for j in range(8):
            row = taps_ref[k : k + 1, 128 * j : 128 * j + 128]
            taps_rows[k, 2 * j : 2 * j + 2, :] = jnp.broadcast_to(row, (2, 128))

    def inputs(start):
        return [s for s in range(start - FILTER_TAPS + 1, start + UNIT) if 0 <= s < FRAMES]

    def filter_antenna(start, a):
        frames = {
            s: x_v[a, slot[s // PIECE] * PIECE + s % PIECE].astype(jnp.float32) for s in inputs(start)
        }
        rows = pl.ds(pl.multiple_of(a * 8, 8), 8)
        for q in range(UNIT):
            total = None
            for k in range(FILTER_TAPS):
                s = start + q - k
                if s in frames:
                    term = taps_rows[k] * frames[s]
                    total = term if total is None else total + term
            if total is None:
                total = jnp.zeros((16, 128), jnp.float32)
            z[0, q, rows, :] = total[:8] + total[8:]
            z[1, q, rows, :] = total[:8] - total[8:]

    def transform(u, odd):
        highs, lows = [], []
        for row in range(8):
            piece = jnp.concatenate(
                [z[odd, e, pl.ds(row, TILE_ANTENNAS, stride=8), :] for e in range(UNIT)], axis=0
            )
            high = piece.astype(jnp.bfloat16)
            highs.append(high)
            lows.append((piece - high.astype(jnp.float32)).astype(jnp.bfloat16))
        high = jnp.concatenate(highs, axis=1)
        low = jnp.concatenate(lows, axis=1)
        count = UNIT * TILE_ANTENNAS
        dot = functools.partial(jnp.dot, preferred_element_type=jnp.float32)
        both = dot(jnp.concatenate([high, low], axis=0), high_ref[odd])
        found = (both[:count] + both[count:] + dot(high, low_ref[odd])).T
        for e in range(UNIT):
            spectra[pl.ds(e, 256, stride=UNIT), :] = found[:, 128 * e : 128 * e + 128]
        for part in range(2):
            rows = spectra[128 * UNIT * part : 128 * UNIT * (part + 1), :]
            out_v[:, odd, part, UNIT * u : UNIT * (u + 1), :] = rows.reshape(DEVICES, UNIT, 128).astype(
                jnp.bfloat16
            )

    leaving = [
        pltpu.make_async_copy(out_v.at[:, odd], out_hbm.at[:, odd], out_sems.at[odd]) for odd in range(2)
    ]
    waited = 0
    for u, start in enumerate(units):
        last = max(slot[s // PIECE] for s in inputs(start))
        while waited <= last:
            copies[waited].wait()
            waited += 1

        def filter_step(a, _, start=start):
            filter_antenna(start, a)
            return 0

        lax.fori_loop(0, TILE_ANTENNAS, filter_step, 0, unroll=2)
        if u == 0:
            for copy in tables:
                copy.wait()
        if u + 1 < len(units):

            def transform_step(odd, _, u=u):
                transform(u, odd)
                return 0

            lax.fori_loop(0, 2, transform_step, 0)
        else:
            for odd in range(2):
                transform(u, odd)
                leaving[odd].start()
    for copy in leaving:
        copy.wait()


def filterbank(frames, taps, high, low, units):
    order = []
    for start in units:
        for s in range(start - FILTER_TAPS + 1, start + UNIT):
            if 0 <= s < FRAMES and s // PIECE not in order:
                order.append(s // PIECE)
    span = UNIT * len(units)
    anywhere = pl.BlockSpec(memory_space=pl.ANY)
    shape = (DEVICES, 2, 2, span, 128)
    table = pltpu.VMEM((2, FRAME_SAMPLES, 256), jnp.bfloat16)
    return pl.pallas_call(
        functools.partial(filterbank_kernel, units, tuple(order)),
        out_shape=jax.ShapeDtypeStruct(shape, jnp.bfloat16),
        in_specs=[anywhere, pl.BlockSpec(memory_space=pltpu.VMEM), anywhere, anywhere],
        out_specs=anywhere,
        scratch_shapes=[
            pltpu.VMEM((TILE_ANTENNAS, PIECE * len(order), 16, 128), jnp.bfloat16),
            pltpu.VMEM((FILTER_TAPS, 16, 128), jnp.float32),
            table,
            table,
            pltpu.VMEM((2, UNIT, 1024, 128), jnp.float32),
            pltpu.VMEM((256 * UNIT, 128), jnp.float32),
            pltpu.VMEM(shape, jnp.bfloat16),
            pltpu.SemaphoreType.DMA((len(order),)),
            pltpu.SemaphoreType.DMA((2,)),
            pltpu.SemaphoreType.DMA((2,)),
        ],
        compiler_params=pltpu.CompilerParams(vmem_limit_bytes=60 * 2**20),
        cost_estimate=pl.CostEstimate(flops=30 * 10**9, bytes_accessed=20 * 2**20, transcendentals=0),
    )(frames, taps, high, low)


def store_left(left, ch, b, block):
    rows = pl.ds(128 * b, 128)
    turned = block.T
    left[ch, 0, rows, :] = turned
    left[ch, 1, rows, 0:DEPTH] = turned[:, DEPTH:]
    left[ch, 1, rows, DEPTH:] = -turned[:, :DEPTH]


def join_kernel(in_ref, y, left):
    def step(ch, _):
        for b in range(ANTENNA_BLOCKS):
            sources, tile = pl.ds((b // 2) * TIME_BLOCKS, TIME_BLOCKS), b % 2
            blocks = []
            for part in range(2):
                early = in_ref[sources, tile, ch, part, 0:8, :].astype(jnp.float32)
                tail = in_ref[sources, tile, ch, part, 8:16, :].astype(jnp.float32)
                rest = in_ref[sources, tile, ch, part, 16:24, :].astype(jnp.float32)
                none = jnp.zeros((1, 8, 128), jnp.float32)
                early = early + jnp.concatenate([none, tail[:-1]], axis=0)
                both = jnp.concatenate([early, rest], axis=1).astype(jnp.bfloat16)
                blocks.append(both.reshape(DEPTH, 128))
            block = jnp.concatenate(blocks, axis=0)
            y[ch, :, 128 * b : 128 * b + 128] = block
            store_left(left, ch, b, block)
        return 0

    lax.fori_loop(0, DEVICE_CHANNELS, step, 0)


def join(received):
    vmem = pl.BlockSpec(memory_space=pltpu.VMEM)
    return pl.pallas_call(
        join_kernel,
        out_shape=(
            jax.ShapeDtypeStruct((DEVICE_CHANNELS, 2 * DEPTH, ANTENNA_COUNT), jnp.bfloat16),
            jax.ShapeDtypeStruct((DEVICE_CHANNELS, 2, ANTENNA_COUNT, 2 * DEPTH), jnp.bfloat16),
        ),
        in_specs=[vmem],
        out_specs=(vmem, vmem),
        compiler_params=pltpu.CompilerParams(vmem_limit_bytes=60 * 2**20),
        cost_estimate=pl.CostEstimate(flops=5 * 10**9, bytes_accessed=12 * 2**20, transcendentals=0),
    )(received)


def correlate_kernel(in_hbm, y_hbm, left_hbm, real_hbm, imag_hbm, *scratch):
    in_ref, y, left, y_old, left_old, tiles, in_sems, old_sems, out_sems = scratch

    def arriving(ch):
        return pltpu.make_async_copy(in_hbm.at[:, :, ch], in_ref.at[:, :, ch], in_sems.at[ch])

    def arriving_old(ch):
        return (
            pltpu.make_async_copy(y_hbm.at[ch], y_old.at[ch], old_sems.at[ch, 0]),
            pltpu.make_async_copy(left_hbm.at[ch], left_old.at[ch], old_sems.at[ch, 1]),
        )

    for ch in range(DEVICE_CHANNELS):
        for copy in (arriving(ch), *arriving_old(ch)):
            copy.start()
    dot = functools.partial(jnp.dot, preferred_element_type=jnp.float32)

    def first(i):
        return ANTENNA_BLOCKS * i - i * (i - 1) // 2

    def prepare(ch):
        for b in range(ANTENNA_BLOCKS):
            sources, tile = pl.ds((b // 2) * TIME_BLOCKS, TIME_BLOCKS), b % 2
            block = jnp.concatenate(
                [in_ref[sources, tile, ch, part, :, :].reshape(DEPTH, 128) for part in range(2)], axis=0
            )
            y[ch, :, 128 * b : 128 * b + 128] = block
            store_left(left, ch, b, block)

    def leaving(ch, pair):
        some = pl.ds(first(2 * pair), first(2 * pair + 2) - first(2 * pair))
        return [
            pltpu.make_async_copy(tiles.at[ch, part, some], ref.at[ch, some], out_sems.at[ch, pair, part])
            for part, ref in enumerate((real_hbm, imag_hbm))
        ]

    def multiply(ch):
        for pair in range(ANTENNA_BLOCKS // 2):
            rows = pl.ds(256 * pair, 256)
            new = left[ch, :, rows, :].reshape(512, 2 * DEPTH)
            old = left_old[ch, :, rows, :].reshape(512, 2 * DEPTH)
            for other in range(pair, ANTENNA_BLOCKS // 2):
                columns = pl.ds(256 * other, 256)
                found = (dot(new, y[ch, :, columns]) + dot(old, y_old[ch, :, columns])) * (1.0 / SPECTRA_COUNT)
                for a in range(2):
                    for b in range(2):
                        i, j = 2 * pair + a, 2 * other + b
                        if i <= j:
                            for part in range(2):
                                top = 256 * part + 128 * a
                                tiles[ch, part, first(i) + j - i] = found[
                                    top : top + 128, 128 * b : 128 * b + 128
                                ]
            for copy in leaving(ch, pair):
                copy.start()

    def step(ch, _):
        arriving(ch).wait()
        prepare(ch)
        for copy in arriving_old(ch):
            copy.wait()
        multiply(ch)
        return 0

    lax.fori_loop(0, DEVICE_CHANNELS, step, 0)
    for ch in range(DEVICE_CHANNELS):
        for pair in range(ANTENNA_BLOCKS // 2):
            for copy in leaving(ch, pair):
                copy.wait()


def correlate(received, y, left):
    out = jax.ShapeDtypeStruct((DEVICE_CHANNELS, PAIRS, 128, 128), jnp.float32)
    anywhere = pl.BlockSpec(memory_space=pl.ANY)
    right_shape = pltpu.VMEM((DEVICE_CHANNELS, 2 * DEPTH, ANTENNA_COUNT), jnp.bfloat16)
    left_shape = pltpu.VMEM((DEVICE_CHANNELS, 2, ANTENNA_COUNT, 2 * DEPTH), jnp.bfloat16)
    return pl.pallas_call(
        correlate_kernel,
        out_shape=(out, out),
        in_specs=[anywhere] * 3,
        out_specs=(anywhere, anywhere),
        scratch_shapes=[
            pltpu.VMEM(received.shape, jnp.bfloat16),
            right_shape,
            left_shape,
            right_shape,
            left_shape,
            pltpu.VMEM((DEVICE_CHANNELS, 2, PAIRS, 128, 128), jnp.float32),
            pltpu.SemaphoreType.DMA((DEVICE_CHANNELS,)),
            pltpu.SemaphoreType.DMA((DEVICE_CHANNELS, 2)),
            pltpu.SemaphoreType.DMA((DEVICE_CHANNELS, ANTENNA_BLOCKS // 2, 2)),
        ],
        compiler_params=pltpu.CompilerParams(vmem_limit_bytes=60 * 2**20),
        cost_estimate=pl.CostEstimate(flops=5 * 10**9, bytes_accessed=12 * 2**20, transcendentals=0),
    )(received, y, left)


def exchange(departing):
    received = lax.all_to_all(departing, AXES, split_axis=0, concat_axis=0, tiled=True)
    return received.reshape(DEVICES // 2, 2, *received.shape[1:])


def on_device(voltages, taps):
    frames = voltages.reshape(TILE_ANTENNAS, FRAMES, 2, 8, 128).transpose(0, 1, 3, 2, 4)
    frames = frames.reshape(TILE_ANTENNAS, FRAMES, 16, 128)
    high, low = (jnp.asarray(table) for table in transform_tables())
    early = filterbank(frames, taps, high, low, EARLY_UNITS)
    taps, early = lax.optimization_barrier((taps, early))
    late = filterbank(frames, taps, high, low, LATE_UNITS)
    y, left = join(exchange(early))
    return correlate(exchange(late), y, left)


def solution(mesh):
    in_specs = (P(("grp", "tile"), "chan", None, None), P())
    out_specs = (P(AXES, None, None, None), P(AXES, None, None, None))
    return jax.shard_map(
        on_device, mesh=mesh, in_specs=in_specs, out_specs=out_specs, check_vma=False
    )
```

```python
import functools

import jax
import jax.numpy as jnp
import ml_dtypes
import numpy as np
from jax import lax
from jax.experimental import pallas as pl
from jax.experimental.pallas import tpu as pltpu
from jax.sharding import PartitionSpec as P

ANTENNA_COUNT = 1024
FRAME_SAMPLES = 1024
FILTER_TAPS = 8
ANTENNA_BLOCKS = 8
SPECTRA_COUNT = 512
DEVICE_CHANNELS = 2
TILE_ANTENNAS = 128
DEVICES = 128
FRAMES = 32
PIECE = 4
TIME_BLOCKS = 16
PAIRS = ANTENNA_BLOCKS * (ANTENNA_BLOCKS + 1) // 2
HALF = FRAME_SAMPLES // 2
AXES = ("grp", "chan", "tile")

EARLY_UNITS = ((0, 8), (32, 8), (8, 4))
LATE_UNITS = ((16, 8), (24, 8), (12, 4))
OLD_DEPTH = 2 * (8 + 4) * TIME_BLOCKS
DEPTH = 2 * FRAMES * TIME_BLOCKS


def transform_tables():
    sample = np.arange(HALF)
    parts = []
    for odd in range(2):
        channel = 2 * np.arange(DEVICES) + odd
        angle = 2.0 * np.pi * ((sample[:, None] * channel[None, :]) % FRAME_SAMPLES) / FRAME_SAMPLES
        cosine, sine = np.cos(angle), np.sin(angle)
        from_real = np.concatenate([cosine, -sine], axis=1)
        from_imag = np.concatenate([sine, cosine], axis=1)
        both = np.stack([from_real.reshape(4, 128, 256), from_imag.reshape(4, 128, 256)], axis=1)
        parts.append(both.reshape(FRAME_SAMPLES, 256))
    table = np.stack(parts).astype(np.float32)
    high = table.astype(ml_dtypes.bfloat16)
    low = (table - high.astype(np.float32)).astype(ml_dtypes.bfloat16)
    return high, low


def filterbank_kernel(units, order, x_hbm, taps_ref, high_hbm, low_hbm, out_hbm, *scratch):
    x_v, taps_rows, high_ref, low_ref, z, spectra, out_v, x_sems, table_sems, out_sems = scratch
    slot = {piece: i for i, piece in enumerate(order)}
    copies = [
        pltpu.make_async_copy(
            x_hbm.at[:, pl.ds(PIECE * piece, PIECE)], x_v.at[:, pl.ds(PIECE * i, PIECE)], x_sems.at[i]
        )
        for i, piece in enumerate(order)
    ]
    tables = [
        pltpu.make_async_copy(high_hbm, high_ref, table_sems.at[0]),
        pltpu.make_async_copy(low_hbm, low_ref, table_sems.at[1]),
    ]
    for copy in copies[:2] + tables + copies[2:]:
        copy.start()
    for k in range(FILTER_TAPS):
        for j in range(8):
            row = taps_ref[k : k + 1, 128 * j : 128 * j + 128]
            taps_rows[k, 2 * j : 2 * j + 2, :] = jnp.broadcast_to(row, (2, 128))

    def inputs(start, count):
        return [s for s in range(start - FILTER_TAPS + 1, start + count) if 0 <= s < FRAMES]

    def filter_antenna(start, count, a):
        frames = {
            s: x_v[a, slot[s // PIECE] * PIECE + s % PIECE].astype(jnp.float32)
            for s in inputs(start, count)
        }
        rows = pl.ds(pl.multiple_of(a * 8, 8), 8)
        for q in range(count):
            total = None
            for k in range(FILTER_TAPS):
                s = start + q - k
                if s in frames:
                    term = taps_rows[k] * frames[s]
                    total = term if total is None else total + term
            if total is None:
                total = jnp.zeros((16, 128), jnp.float32)
            z[0, q, rows, :] = total[:8] + total[8:]
            z[1, q, rows, :] = total[:8] - total[8:]

    def transform(count, top, odd):
        highs, lows = [], []
        for row in range(8):
            piece = jnp.concatenate(
                [z[odd, e, pl.ds(row, TILE_ANTENNAS, stride=8), :] for e in range(count)], axis=0
            )
            high = piece.astype(jnp.bfloat16)
            highs.append(high)
            lows.append((piece - high.astype(jnp.float32)).astype(jnp.bfloat16))
        high = jnp.concatenate(highs, axis=1)
        low = jnp.concatenate(lows, axis=1)
        size = count * TILE_ANTENNAS
        dot = functools.partial(jnp.dot, preferred_element_type=jnp.float32)
        both = dot(jnp.concatenate([high, low], axis=0), high_ref[odd])
        found = (both[:size] + both[size:] + dot(high, low_ref[odd])).T
        step = 1024 if count == 8 else 4
        for part in range(2):
            for e in range(count):
                spectra[pl.ds(step * part + e, DEVICES, stride=8), :] = found[
                    128 * part : 128 * part + 128, 128 * e : 128 * e + 128
                ]
        for n in range(count // 4):
            rows = spectra[1024 * n : 1024 * (n + 1), :].reshape(DEVICES, 8, 128)
            place = top + 2 * count * odd + 8 * n
            out_v[:, place : place + 8, :] = rows.astype(jnp.bfloat16)

    waited = 0
    top = 0
    leaving = []
    for u, (start, count) in enumerate(units):
        last = max(slot[s // PIECE] for s in inputs(start, count))
        while waited <= last:
            copies[waited].wait()
            waited += 1

        def filter_step(a, _, start=start, count=count):
            filter_antenna(start, count, a)
            return 0

        lax.fori_loop(0, TILE_ANTENNAS, filter_step, 0, unroll=2)
        if u == 0:
            for copy in tables:
                copy.wait()
        for odd in range(2):
            transform(count, top, odd)
        rows = pl.ds(top, 4 * count)
        copy = pltpu.make_async_copy(out_v.at[:, rows], out_hbm.at[:, rows], out_sems.at[u])
        copy.start()
        leaving.append(copy)
        top += 4 * count
    for copy in leaving:
        copy.wait()


def filterbank(frames, taps, high, low, units):
    order = []
    for start, count in units:
        for s in range(start - FILTER_TAPS + 1, start + count):
            if 0 <= s < FRAMES and s // PIECE not in order:
                order.append(s // PIECE)
    anywhere = pl.BlockSpec(memory_space=pl.ANY)
    shape = (DEVICES, 4 * sum(count for _, count in units), 128)
    table = pltpu.VMEM((2, FRAME_SAMPLES, 256), jnp.bfloat16)
    return pl.pallas_call(
        functools.partial(filterbank_kernel, units, tuple(order)),
        out_shape=jax.ShapeDtypeStruct(shape, jnp.bfloat16),
        in_specs=[anywhere, pl.BlockSpec(memory_space=pltpu.VMEM), anywhere, anywhere],
        out_specs=anywhere,
        scratch_shapes=[
            pltpu.VMEM((TILE_ANTENNAS, PIECE * len(order), 16, 128), jnp.bfloat16),
            pltpu.VMEM((FILTER_TAPS, 16, 128), jnp.float32),
            table,
            table,
            pltpu.VMEM((2, 8, 1024, 128), jnp.float32),
            pltpu.VMEM((2048, 128), jnp.float32),
            pltpu.VMEM(shape, jnp.bfloat16),
            pltpu.SemaphoreType.DMA((len(order),)),
            pltpu.SemaphoreType.DMA((2,)),
            pltpu.SemaphoreType.DMA((len(units),)),
        ],
        compiler_params=pltpu.CompilerParams(vmem_limit_bytes=60 * 2**20),
        cost_estimate=pl.CostEstimate(flops=30 * 10**9, bytes_accessed=20 * 2**20, transcendentals=0),
    )(frames, taps, high, low)


def store_eight(y, left, b, depth, real, imag):
    rows, half, end = slice(128 * b, 128 * b + 128), depth + 128, depth + 256
    parts = [part.reshape(8 * TIME_BLOCKS, 128).astype(jnp.bfloat16) for part in (real, imag)]
    block = jnp.concatenate(parts, axis=0)
    turned = block.T
    y[depth:end, rows] = block
    left[0, rows, depth:end] = turned
    left[1, rows, depth:half] = turned[:, 128:]
    left[1, rows, half:end] = -turned[:, :128]


def store_four(y, left, b, depth, both):
    rows, end = slice(128 * b, 128 * b + 128), depth + 128
    swapped = jnp.concatenate([both[:, 4:], -both[:, :4]], axis=1)
    block, swapped = (
        part.reshape(8 * TIME_BLOCKS, 128).astype(jnp.bfloat16) for part in (both, swapped)
    )
    y[depth:end, rows] = block
    left[0, rows, depth:end] = block.T
    left[1, rows, depth:end] = swapped.T


def join_kernel(in_ref, y, left):
    for ch in range(DEVICE_CHANNELS):
        for b in range(ANTENNA_BLOCKS):
            sources, tile = pl.ds((b // 2) * TIME_BLOCKS, TIME_BLOCKS), b % 2

            def eight(row):
                return in_ref[sources, tile, row : row + 8, :].astype(jnp.float32)

            parts = []
            for part in range(2):
                tail = eight(32 + 16 * ch + 8 * part)
                none = jnp.zeros((1, 8, 128), jnp.float32)
                parts.append(eight(16 * ch + 8 * part) + jnp.concatenate([none, tail[:-1]], axis=0))
            store_eight(y.at[ch], left.at[ch], b, 0, *parts)
            store_four(y.at[ch], left.at[ch], b, 256, eight(64 + 8 * ch))


def join(received):
    vmem = pl.BlockSpec(memory_space=pltpu.VMEM)
    return pl.pallas_call(
        join_kernel,
        out_shape=(
            jax.ShapeDtypeStruct((DEVICE_CHANNELS, OLD_DEPTH, ANTENNA_COUNT), jnp.bfloat16),
            jax.ShapeDtypeStruct((DEVICE_CHANNELS, 2, ANTENNA_COUNT, OLD_DEPTH), jnp.bfloat16),
        ),
        in_specs=[vmem],
        out_specs=(vmem, vmem),
        compiler_params=pltpu.CompilerParams(vmem_limit_bytes=24 * 2**20),
        cost_estimate=pl.CostEstimate(flops=5 * 10**9, bytes_accessed=12 * 2**20, transcendentals=0),
    )(received)


def correlate_kernel(in_hbm, y_hbm, left_hbm, real_hbm, imag_hbm, *scratch):
    in_ref, y, left, tiles, in_sem, old_sems, out_sems = scratch
    arriving = pltpu.make_async_copy(in_hbm, in_ref, in_sem)

    def arriving_old(ch):
        old = pl.ds(0, OLD_DEPTH)
        return (
            pltpu.make_async_copy(y_hbm.at[ch], y.at[ch, old], old_sems.at[ch, 0]),
            pltpu.make_async_copy(left_hbm.at[ch], left.at[ch, :, :, old], old_sems.at[ch, 1]),
        )

    arriving.start()
    for ch in range(DEVICE_CHANNELS):
        for copy in arriving_old(ch):
            copy.start()
    dot = functools.partial(jnp.dot, preferred_element_type=jnp.float32)

    def first(i):
        return ANTENNA_BLOCKS * i - i * (i - 1) // 2

    def prepare(ch):
        for b in range(ANTENNA_BLOCKS):
            sources, tile = pl.ds((b // 2) * TIME_BLOCKS, TIME_BLOCKS), b % 2

            def eight(row):
                return in_ref[sources, tile, row : row + 8, :].astype(jnp.float32)

            for unit in range(2):
                row = 32 * unit + 16 * ch
                store_eight(y.at[ch], left.at[ch], b, OLD_DEPTH + 256 * unit, eight(row), eight(row + 8))
            store_four(y.at[ch], left.at[ch], b, OLD_DEPTH + 512, eight(64 + 8 * ch))

    def leaving(ch, pair):
        some = pl.ds(first(2 * pair), first(2 * pair + 2) - first(2 * pair))
        return [
            pltpu.make_async_copy(tiles.at[ch, part, some], ref.at[ch, some], out_sems.at[ch, pair, part])
            for part, ref in enumerate((real_hbm, imag_hbm))
        ]

    def multiply(ch):
        for pair in range(ANTENNA_BLOCKS // 2):
            rows = pl.ds(256 * pair, 256)
            lhs = left[ch, :, rows, :].reshape(512, DEPTH)
            for other in range(pair, ANTENNA_BLOCKS // 2):
                columns = pl.ds(256 * other, 256)
                found = dot(lhs, y[ch, :, columns]) * (1.0 / SPECTRA_COUNT)
                for a in range(2):
                    for b in range(2):
                        i, j = 2 * pair + a, 2 * other + b
                        if i <= j:
                            for part in range(2):
                                top = 256 * part + 128 * a
                                tiles[ch, part, first(i) + j - i] = found[
                                    top : top + 128, 128 * b : 128 * b + 128
                                ]
            for copy in leaving(ch, pair):
                copy.start()

    def step(ch, _):
        for copy in arriving_old(ch):
            copy.wait()
        multiply(ch)
        return 0

    arriving.wait()
    for ch in range(DEVICE_CHANNELS):
        prepare(ch)
    lax.fori_loop(0, DEVICE_CHANNELS, step, 0)
    for ch in range(DEVICE_CHANNELS):
        for pair in range(ANTENNA_BLOCKS // 2):
            for copy in leaving(ch, pair):
                copy.wait()


def correlate(received, y, left):
    out = jax.ShapeDtypeStruct((DEVICE_CHANNELS, PAIRS, 128, 128), jnp.float32)
    anywhere = pl.BlockSpec(memory_space=pl.ANY)
    return pl.pallas_call(
        correlate_kernel,
        out_shape=(out, out),
        in_specs=[anywhere] * 3,
        out_specs=(anywhere, anywhere),
        scratch_shapes=[
            pltpu.VMEM(received.shape, jnp.bfloat16),
            pltpu.VMEM((DEVICE_CHANNELS, DEPTH, ANTENNA_COUNT), jnp.bfloat16),
            pltpu.VMEM((DEVICE_CHANNELS, 2, ANTENNA_COUNT, DEPTH), jnp.bfloat16),
            pltpu.VMEM((DEVICE_CHANNELS, 2, PAIRS, 128, 128), jnp.float32),
            pltpu.SemaphoreType.DMA,
            pltpu.SemaphoreType.DMA((DEVICE_CHANNELS, 2)),
            pltpu.SemaphoreType.DMA((DEVICE_CHANNELS, ANTENNA_BLOCKS // 2, 2)),
        ],
        compiler_params=pltpu.CompilerParams(vmem_limit_bytes=60 * 2**20),
        cost_estimate=pl.CostEstimate(flops=5 * 10**9, bytes_accessed=12 * 2**20, transcendentals=0),
    )(received, y, left)


def exchange(departing):
    received = lax.all_to_all(departing, AXES, split_axis=0, concat_axis=0, tiled=True)
    return received.reshape(DEVICES // 2, 2, *received.shape[1:])


def on_device(voltages, taps):
    frames = voltages.reshape(TILE_ANTENNAS, FRAMES, 2, 8, 128).transpose(0, 1, 3, 2, 4)
    frames = frames.reshape(TILE_ANTENNAS, FRAMES, 16, 128)
    high, low = (jnp.asarray(table) for table in transform_tables())
    early = filterbank(frames, taps, high, low, EARLY_UNITS)
    taps, early = lax.optimization_barrier((taps, early))
    late = filterbank(frames, taps, high, low, LATE_UNITS)
    y, left = join(exchange(early))
    return correlate(exchange(late), y, left)


def solution(mesh):
    in_specs = (P(("grp", "tile"), "chan", None, None), P())
    out_specs = (P(AXES, None, None, None), P(AXES, None, None, None))
    return jax.shard_map(
        on_device, mesh=mesh, in_specs=in_specs, out_specs=out_specs, check_vma=False
    )
```

```python
import functools

import jax
import jax.numpy as jnp
import ml_dtypes
import numpy as np
from jax import lax
from jax.experimental import pallas as pl
from jax.experimental.pallas import tpu as pltpu
from jax.sharding import PartitionSpec as P

ANTENNA_COUNT = 1024
FRAME_SAMPLES = 1024
FILTER_TAPS = 8
ANTENNA_BLOCKS = 8
SPECTRA_COUNT = 512
DEVICE_CHANNELS = 2
TILE_ANTENNAS = 128
DEVICES = 128
FRAMES = 32
PIECE = 4
TIME_BLOCKS = 16
PAIRS = ANTENNA_BLOCKS * (ANTENNA_BLOCKS + 1) // 2
HALF = FRAME_SAMPLES // 2
AXES = ("grp", "chan", "tile")
SHARES = 4
SHARE = TILE_ANTENNAS // SHARES

EARLY_UNITS = ((0, 8), (32, 8), (8, 4))
LATE_UNITS = ((16, 8), (24, 8), (12, 4))
OLD_DEPTH = 2 * (8 + 4) * TIME_BLOCKS
DEPTH = 2 * FRAMES * TIME_BLOCKS


def transform_tables():
    sample = np.arange(HALF)
    parts = []
    for odd in range(2):
        channel = 2 * np.arange(DEVICES) + odd
        angle = 2.0 * np.pi * ((sample[:, None] * channel[None, :]) % FRAME_SAMPLES) / FRAME_SAMPLES
        cosine, sine = np.cos(angle), np.sin(angle)
        from_real = np.concatenate([cosine, -sine], axis=1)
        from_imag = np.concatenate([sine, cosine], axis=1)
        both = np.stack([from_real.reshape(4, 128, 256), from_imag.reshape(4, 128, 256)], axis=1)
        parts.append(both.reshape(FRAME_SAMPLES, 256))
    table = np.stack(parts).astype(np.float32)
    high = table.astype(ml_dtypes.bfloat16)
    low = (table - high.astype(np.float32)).astype(ml_dtypes.bfloat16)
    return high, low


def filterbank_kernel(units, order, x_hbm, taps_ref, high_hbm, low_hbm, out_hbm, *scratch):
    x_v, taps_rows, high_ref, low_ref, z, spectra, out_v, x_sems, table_sems, out_sems = scratch
    slot = {piece: i for i, piece in enumerate(order)}

    def arriving(i, share):
        antennas = pl.ds(SHARE * share, SHARE)
        return pltpu.make_async_copy(
            x_hbm.at[antennas, pl.ds(PIECE * order[i], PIECE)],
            x_v.at[antennas, pl.ds(PIECE * i, PIECE)],
            x_sems.at[i, share],
        )

    tables = [
        pltpu.make_async_copy(high_hbm, high_ref, table_sems.at[0]),
        pltpu.make_async_copy(low_hbm, low_ref, table_sems.at[1]),
    ]
    for share in range(SHARES):
        for i in range(2):
            arriving(i, share).start()
    for copy in tables:
        copy.start()
    for i in range(2, len(order)):
        for share in range(SHARES):
            arriving(i, share).start()
    for k in range(FILTER_TAPS):
        for j in range(8):
            row = taps_ref[k : k + 1, 128 * j : 128 * j + 128]
            taps_rows[k, 2 * j : 2 * j + 2, :] = jnp.broadcast_to(row, (2, 128))

    def inputs(start, count):
        return [s for s in range(start - FILTER_TAPS + 1, start + count) if 0 <= s < FRAMES]

    def filter_antenna(start, count, group, k8):
        a = group * 8 + k8
        frames = {
            s: x_v[a, slot[s // PIECE] * PIECE + s % PIECE].astype(jnp.float32)
            for s in inputs(start, count)
        }
        rows = pl.ds(pl.multiple_of(group * 64, 64) + k8, 8, stride=8)
        for q in range(count):
            total = None
            for k in range(FILTER_TAPS):
                s = start + q - k
                if s in frames:
                    term = taps_rows[k] * frames[s]
                    total = term if total is None else total + term
            if total is None:
                total = jnp.zeros((16, 128), jnp.float32)
            z[0, q, rows, :] = total[:8] + total[8:]
            z[1, q, rows, :] = total[:8] - total[8:]

    def transform(count, top, odd):
        highs, lows = [], []
        for row in range(8):
            piece = jnp.concatenate(
                [
                    z[odd, e].reshape(TILE_ANTENNAS // 8, 8, 8, 128)[:, row].reshape(TILE_ANTENNAS, 128)
                    for e in range(count)
                ],
                axis=0,
            )
            high = piece.astype(jnp.bfloat16)
            highs.append(high)
            lows.append((piece - high.astype(jnp.float32)).astype(jnp.bfloat16))
        high = jnp.concatenate(highs, axis=1)
        low = jnp.concatenate(lows, axis=1)
        size = count * TILE_ANTENNAS
        dot = functools.partial(jnp.dot, preferred_element_type=jnp.float32)
        both = dot(jnp.concatenate([high, low], axis=0), high_ref[odd])
        found = (both[:size] + both[size:] + dot(high, low_ref[odd])).T
        step = 1024 if count == 8 else 4
        for part in range(2):
            for e in range(count):
                spectra[pl.ds(step * part + e, DEVICES, stride=8), :] = found[
                    128 * part : 128 * part + 128, 128 * e : 128 * e + 128
                ]
        for n in range(count // 4):
            rows = spectra[1024 * n : 1024 * (n + 1), :].reshape(DEVICES, 8, 128)
            place = top + 2 * count * odd + 8 * n
            out_v[:, place : place + 8, :] = rows.astype(jnp.bfloat16)

    waited = 0
    top = 0
    leaving = []
    for u, (start, count) in enumerate(units):
        last = max(slot[s // PIECE] for s in inputs(start, count))

        def filter_step(group, _, start=start, count=count):
            for k8 in range(8):
                filter_antenna(start, count, group, k8)
            return 0

        def filter_share(share, _, last=last, waited=waited, filter_step=filter_step):
            for i in range(waited, last + 1):
                arriving(i, share).wait()
            lax.fori_loop(0, SHARE // 8, lambda n, c: filter_step(SHARE // 8 * share + n, c), 0)
            return 0

        if waited <= last:
            lax.fori_loop(0, SHARES, filter_share, 0)
            waited = last + 1
        else:
            lax.fori_loop(0, TILE_ANTENNAS // 8, filter_step, 0)
        if u == 0:
            for copy in tables:
                copy.wait()
        for odd in range(2):
            transform(count, top, odd)
        rows = pl.ds(top, 4 * count)
        copy = pltpu.make_async_copy(out_v.at[:, rows], out_hbm.at[:, rows], out_sems.at[u])
        copy.start()
        leaving.append(copy)
        top += 4 * count
    for copy in leaving:
        copy.wait()


def filterbank(frames, taps, high, low, units):
    order = []
    for start, count in units:
        for s in range(start - FILTER_TAPS + 1, start + count):
            if 0 <= s < FRAMES and s // PIECE not in order:
                order.append(s // PIECE)
    anywhere = pl.BlockSpec(memory_space=pl.ANY)
    shape = (DEVICES, 4 * sum(count for _, count in units), 128)
    table = pltpu.VMEM((2, FRAME_SAMPLES, 256), jnp.bfloat16)
    return pl.pallas_call(
        functools.partial(filterbank_kernel, units, tuple(order)),
        out_shape=jax.ShapeDtypeStruct(shape, jnp.bfloat16),
        in_specs=[anywhere, pl.BlockSpec(memory_space=pltpu.VMEM), anywhere, anywhere],
        out_specs=anywhere,
        scratch_shapes=[
            pltpu.VMEM((TILE_ANTENNAS, PIECE * len(order), 16, 128), jnp.bfloat16),
            pltpu.VMEM((FILTER_TAPS, 16, 128), jnp.float32),
            table,
            table,
            pltpu.VMEM((2, 8, 1024, 128), jnp.float32),
            pltpu.VMEM((2048, 128), jnp.float32),
            pltpu.VMEM(shape, jnp.bfloat16),
            pltpu.SemaphoreType.DMA((len(order), SHARES)),
            pltpu.SemaphoreType.DMA((2,)),
            pltpu.SemaphoreType.DMA((len(units),)),
        ],
        compiler_params=pltpu.CompilerParams(vmem_limit_bytes=60 * 2**20),
        cost_estimate=pl.CostEstimate(flops=30 * 10**9, bytes_accessed=20 * 2**20, transcendentals=0),
    )(frames, taps, high, low)


def store_eight(y, left, b, depth, real, imag):
    rows, half, end = slice(128 * b, 128 * b + 128), depth + 128, depth + 256
    parts = [part.reshape(8 * TIME_BLOCKS, 128).astype(jnp.bfloat16) for part in (real, imag)]
    block = jnp.concatenate(parts, axis=0)
    turned = block.T
    y[depth:end, rows] = block
    left[0, rows, depth:end] = turned
    left[1, rows, depth:half] = turned[:, 128:]
    left[1, rows, half:end] = -turned[:, :128]


def store_four(y, left, b, depth, both):
    rows, end = slice(128 * b, 128 * b + 128), depth + 128
    swapped = jnp.concatenate([both[:, 4:], -both[:, :4]], axis=1)
    block, swapped = (
        part.reshape(8 * TIME_BLOCKS, 128).astype(jnp.bfloat16) for part in (both, swapped)
    )
    y[depth:end, rows] = block
    left[0, rows, depth:end] = block.T
    left[1, rows, depth:end] = swapped.T


def join_kernel(in_ref, y, left):
    for ch in range(DEVICE_CHANNELS):
        for b in range(ANTENNA_BLOCKS):
            sources, tile = pl.ds((b // 2) * TIME_BLOCKS, TIME_BLOCKS), b % 2

            def eight(row):
                return in_ref[sources, tile, row : row + 8, :].astype(jnp.float32)

            parts = []
            for part in range(2):
                tail = eight(32 + 16 * ch + 8 * part)
                none = jnp.zeros((1, 8, 128), jnp.float32)
                parts.append(eight(16 * ch + 8 * part) + jnp.concatenate([none, tail[:-1]], axis=0))
            store_eight(y.at[ch], left.at[ch], b, 0, *parts)
            store_four(y.at[ch], left.at[ch], b, 256, eight(64 + 8 * ch))


def join(received):
    vmem = pl.BlockSpec(memory_space=pltpu.VMEM)
    return pl.pallas_call(
        join_kernel,
        out_shape=(
            jax.ShapeDtypeStruct((DEVICE_CHANNELS, OLD_DEPTH, ANTENNA_COUNT), jnp.bfloat16),
            jax.ShapeDtypeStruct((DEVICE_CHANNELS, 2, ANTENNA_COUNT, OLD_DEPTH), jnp.bfloat16),
        ),
        in_specs=[vmem],
        out_specs=(vmem, vmem),
        compiler_params=pltpu.CompilerParams(vmem_limit_bytes=24 * 2**20),
        cost_estimate=pl.CostEstimate(flops=5 * 10**9, bytes_accessed=12 * 2**20, transcendentals=0),
    )(received)


def correlate_kernel(in_hbm, y_hbm, left_hbm, real_hbm, imag_hbm, *scratch):
    in_ref, y, left, tiles, in_sems, old_sems, out_sems = scratch

    def arriving(ch):
        tops = (0, 32, 64) if ch == 0 else (16, 48)
        return [
            pltpu.make_async_copy(
                in_hbm.at[:, :, pl.ds(top, 16)], in_ref.at[:, :, pl.ds(top, 16)], in_sems.at[top // 16]
            )
            for top in tops
        ]

    def arriving_old(ch):
        old = pl.ds(0, OLD_DEPTH)
        return (
            pltpu.make_async_copy(y_hbm.at[ch], y.at[ch, old], old_sems.at[ch, 0]),
            pltpu.make_async_copy(left_hbm.at[ch], left.at[ch, :, :, old], old_sems.at[ch, 1]),
        )

    for ch in range(DEVICE_CHANNELS):
        for copy in (*arriving(ch), *arriving_old(ch)):
            copy.start()
    dot = functools.partial(jnp.dot, preferred_element_type=jnp.float32)

    def first(i):
        return ANTENNA_BLOCKS * i - i * (i - 1) // 2

    def prepare(ch):
        for b in range(ANTENNA_BLOCKS):
            sources, tile = pl.ds((b // 2) * TIME_BLOCKS, TIME_BLOCKS), b % 2

            def eight(row):
                return in_ref[sources, tile, row : row + 8, :].astype(jnp.float32)

            for unit in range(2):
                row = 32 * unit + 16 * ch
                store_eight(y.at[ch], left.at[ch], b, OLD_DEPTH + 256 * unit, eight(row), eight(row + 8))
            store_four(y.at[ch], left.at[ch], b, OLD_DEPTH + 512, eight(64 + 8 * ch))

    def leaving(ch, pair):
        some = pl.ds(first(2 * pair), first(2 * pair + 2) - first(2 * pair))
        return [
            pltpu.make_async_copy(tiles.at[ch, part, some], ref.at[ch, some], out_sems.at[ch, pair, part])
            for part, ref in enumerate((real_hbm, imag_hbm))
        ]

    def multiply(ch):
        for pair in range(ANTENNA_BLOCKS // 2):
            rows = pl.ds(256 * pair, 256)
            lhs = left[ch, :, rows, :].reshape(512, DEPTH)
            for other in range(pair, ANTENNA_BLOCKS // 2):
                columns = pl.ds(256 * other, 256)
                found = dot(lhs, y[ch, :, columns]) * (1.0 / SPECTRA_COUNT)
                for a in range(2):
                    for b in range(2):
                        i, j = 2 * pair + a, 2 * other + b
                        if i <= j:
                            for part in range(2):
                                top = 256 * part + 128 * a
                                tiles[ch, part, first(i) + j - i] = found[
                                    top : top + 128, 128 * b : 128 * b + 128
                                ]
            for copy in leaving(ch, pair):
                copy.start()

    for ch in range(DEVICE_CHANNELS):
        for copy in arriving(ch):
            copy.wait()
        prepare(ch)
        for copy in arriving_old(ch):
            copy.wait()
        multiply(ch)
    for ch in range(DEVICE_CHANNELS):
        for pair in range(ANTENNA_BLOCKS // 2):
            for copy in leaving(ch, pair):
                copy.wait()


def correlate(received, y, left):
    out = jax.ShapeDtypeStruct((DEVICE_CHANNELS, PAIRS, 128, 128), jnp.float32)
    anywhere = pl.BlockSpec(memory_space=pl.ANY)
    return pl.pallas_call(
        correlate_kernel,
        out_shape=(out, out),
        in_specs=[anywhere] * 3,
        out_specs=(anywhere, anywhere),
        scratch_shapes=[
            pltpu.VMEM(received.shape, jnp.bfloat16),
            pltpu.VMEM((DEVICE_CHANNELS, DEPTH, ANTENNA_COUNT), jnp.bfloat16),
            pltpu.VMEM((DEVICE_CHANNELS, 2, ANTENNA_COUNT, DEPTH), jnp.bfloat16),
            pltpu.VMEM((DEVICE_CHANNELS, 2, PAIRS, 128, 128), jnp.float32),
            pltpu.SemaphoreType.DMA((5,)),
            pltpu.SemaphoreType.DMA((DEVICE_CHANNELS, 2)),
            pltpu.SemaphoreType.DMA((DEVICE_CHANNELS, ANTENNA_BLOCKS // 2, 2)),
        ],
        compiler_params=pltpu.CompilerParams(vmem_limit_bytes=60 * 2**20),
        cost_estimate=pl.CostEstimate(flops=5 * 10**9, bytes_accessed=12 * 2**20, transcendentals=0),
    )(received, y, left)


def exchange(departing):
    received = lax.all_to_all(departing, AXES, split_axis=0, concat_axis=0, tiled=True)
    return received.reshape(DEVICES // 2, 2, *received.shape[1:])


def on_device(voltages, taps):
    frames = voltages.reshape(TILE_ANTENNAS, FRAMES, 2, 8, 128).transpose(0, 1, 3, 2, 4)
    frames = frames.reshape(TILE_ANTENNAS, FRAMES, 16, 128)
    high, low = (jnp.asarray(table) for table in transform_tables())
    early = filterbank(frames, taps, high, low, EARLY_UNITS)
    taps, early = lax.optimization_barrier((taps, early))
    late = filterbank(frames, taps, high, low, LATE_UNITS)
    y, left = join(exchange(early))
    return correlate(exchange(late), y, left)


def solution(mesh):
    in_specs = (P(("grp", "tile"), "chan", None, None), P())
    out_specs = (P(AXES, None, None, None), P(AXES, None, None, None))
    return jax.shard_map(
        on_device, mesh=mesh, in_specs=in_specs, out_specs=out_specs, check_vma=False
    )
```

```python
import functools

import jax
import jax.numpy as jnp
import ml_dtypes
import numpy as np
from jax import lax
from jax.experimental import pallas as pl
from jax.experimental.pallas import tpu as pltpu
from jax.sharding import PartitionSpec as P

ANTENNA_COUNT = 1024
FRAME_SAMPLES = 1024
FILTER_TAPS = 8
ANTENNA_BLOCKS = 8
SPECTRA_COUNT = 512
DEVICE_CHANNELS = 2
TILE_ANTENNAS = 128
DEVICES = 128
FRAMES = 32
PIECE = 4
TIME_BLOCKS = 16
PAIRS = ANTENNA_BLOCKS * (ANTENNA_BLOCKS + 1) // 2
HALF = FRAME_SAMPLES // 2
AXES = ("grp", "chan", "tile")
SHARES = 4
SHARE = TILE_ANTENNAS // SHARES

EARLY_UNITS = ((0, 8), (32, 8), (8, 4))
LATE_UNITS = ((16, 8), (24, 8), (12, 4))
OLD_DEPTH = 2 * (8 + 4) * TIME_BLOCKS
DEPTH = 2 * FRAMES * TIME_BLOCKS


def transform_tables():
    sample = np.arange(HALF)
    parts = []
    for odd in range(2):
        channel = 2 * np.arange(DEVICES) + odd
        angle = 2.0 * np.pi * ((sample[:, None] * channel[None, :]) % FRAME_SAMPLES) / FRAME_SAMPLES
        cosine, sine = np.cos(angle), np.sin(angle)
        from_real = np.concatenate([cosine, -sine], axis=1)
        from_imag = np.concatenate([sine, cosine], axis=1)
        both = np.stack([from_real.reshape(4, 128, 256), from_imag.reshape(4, 128, 256)], axis=1)
        parts.append(both.reshape(FRAME_SAMPLES, 256))
    table = np.stack(parts).astype(np.float32)
    high = table.astype(ml_dtypes.bfloat16)
    low = (table - high.astype(np.float32)).astype(ml_dtypes.bfloat16)
    return high, low


def filterbank_kernel(units, order, x_hbm, taps_ref, high_hbm, low_hbm, out_hbm, *scratch):
    x_v, taps_rows, high_ref, low_ref, z, spectra, out_v, x_sems, table_sems, out_sems = scratch
    slot = {piece: i for i, piece in enumerate(order)}

    def arriving(i, share):
        antennas = pl.ds(SHARE * share, SHARE)
        return pltpu.make_async_copy(
            x_hbm.at[antennas, pl.ds(PIECE * order[i], PIECE)],
            x_v.at[antennas, pl.ds(PIECE * i, PIECE)],
            x_sems.at[i, share],
        )

    tables = [
        pltpu.make_async_copy(high_hbm, high_ref, table_sems.at[0]),
        pltpu.make_async_copy(low_hbm, low_ref, table_sems.at[1]),
    ]
    for share in range(SHARES):
        for i in range(2):
            arriving(i, share).start()
    for copy in tables:
        copy.start()
    for i in range(2, len(order)):
        for share in range(SHARES):
            arriving(i, share).start()
    for k in range(FILTER_TAPS):
        for j in range(8):
            row = taps_ref[k : k + 1, 128 * j : 128 * j + 128]
            taps_rows[k, 2 * j : 2 * j + 2, :] = jnp.broadcast_to(row, (2, 128))

    def inputs(start, count):
        return [s for s in range(start - FILTER_TAPS + 1, start + count) if 0 <= s < FRAMES]

    def filter_antenna(start, count, place, group, k8):
        a = group * 8 + k8
        frames = {
            s: x_v[a, slot[s // PIECE] * PIECE + s % PIECE].astype(jnp.float32)
            for s in inputs(start, count)
        }
        rows = pl.ds(pl.multiple_of(group * 64, 64) + k8, 8, stride=8)
        for q in range(count):
            total = None
            for k in range(FILTER_TAPS):
                s = start + q - k
                if s in frames:
                    term = taps_rows[k] * frames[s]
                    total = term if total is None else total + term
            if total is None:
                total = jnp.zeros((16, 128), jnp.float32)
            z[0, place + q, rows, :] = total[:8] + total[8:]
            z[1, place + q, rows, :] = total[:8] - total[8:]

    def transform(count, place, odd):
        top = 4 * place
        highs, lows = [], []
        for row in range(8):
            piece = jnp.concatenate(
                [
                    z[odd, place + e].reshape(TILE_ANTENNAS // 8, 8, 8, 128)[:, row].reshape(TILE_ANTENNAS, 128)
                    for e in range(count)
                ],
                axis=0,
            )
            high = piece.astype(jnp.bfloat16)
            highs.append(high)
            lows.append((piece - high.astype(jnp.float32)).astype(jnp.bfloat16))
        high = jnp.concatenate(highs, axis=1)
        low = jnp.concatenate(lows, axis=1)
        size = count * TILE_ANTENNAS
        dot = functools.partial(jnp.dot, preferred_element_type=jnp.float32)
        both = dot(jnp.concatenate([high, low], axis=0), high_ref[odd])
        found = (both[:size] + both[size:] + dot(high, low_ref[odd])).T
        step = 1024 if count == 8 else 4
        for part in range(2):
            for e in range(count):
                spectra[odd, pl.ds(step * part + e, DEVICES, stride=8), :] = found[
                    128 * part : 128 * part + 128, 128 * e : 128 * e + 128
                ]
        for n in range(count // 4):
            rows = spectra[odd, 1024 * n : 1024 * (n + 1), :].reshape(DEVICES, 8, 128)
            row = top + 2 * count * odd + 8 * n
            out_v[:, row : row + 8, :] = rows.astype(jnp.bfloat16)

    waited = 0
    place = 0
    leaving = []
    for u, (start, count) in enumerate(units):
        last = max(slot[s // PIECE] for s in inputs(start, count))

        def filter_step(group, _, start=start, count=count, place=place):
            for k8 in range(8):
                filter_antenna(start, count, place, group, k8)
            return 0

        def filter_share(share, _, last=last, waited=waited, filter_step=filter_step):
            for i in range(waited, last + 1):
                arriving(i, share).wait()
            lax.fori_loop(0, SHARE // 8, lambda n, c: filter_step(SHARE // 8 * share + n, c), 0)
            return 0

        if waited <= last:
            lax.fori_loop(0, SHARES, filter_share, 0)
            waited = last + 1
        else:
            lax.fori_loop(0, TILE_ANTENNAS // 8, filter_step, 0)
        place += count
    for copy in tables:
        copy.wait()
    place = 0
    for u, (start, count) in enumerate(units):
        for odd in range(2):
            transform(count, place, odd)
        rows = pl.ds(4 * place, 4 * count)
        copy = pltpu.make_async_copy(out_v.at[:, rows], out_hbm.at[:, rows], out_sems.at[u])
        copy.start()
        leaving.append(copy)
        place += count
    for copy in leaving:
        copy.wait()


def filterbank(frames, taps, high, low, units):
    order = []
    for start, count in units:
        for s in range(start - FILTER_TAPS + 1, start + count):
            if 0 <= s < FRAMES and s // PIECE not in order:
                order.append(s // PIECE)
    anywhere = pl.BlockSpec(memory_space=pl.ANY)
    shape = (DEVICES, 4 * sum(count for _, count in units), 128)
    table = pltpu.VMEM((2, FRAME_SAMPLES, 256), jnp.bfloat16)
    return pl.pallas_call(
        functools.partial(filterbank_kernel, units, tuple(order)),
        out_shape=jax.ShapeDtypeStruct(shape, jnp.bfloat16),
        in_specs=[anywhere, pl.BlockSpec(memory_space=pltpu.VMEM), anywhere, anywhere],
        out_specs=anywhere,
        scratch_shapes=[
            pltpu.VMEM((TILE_ANTENNAS, PIECE * len(order), 16, 128), jnp.bfloat16),
            pltpu.VMEM((FILTER_TAPS, 16, 128), jnp.float32),
            table,
            table,
            pltpu.VMEM((2, shape[1] // 4, 1024, 128), jnp.float32),
            pltpu.VMEM((2, 2048, 128), jnp.float32),
            pltpu.VMEM(shape, jnp.bfloat16),
            pltpu.SemaphoreType.DMA((len(order), SHARES)),
            pltpu.SemaphoreType.DMA((2,)),
            pltpu.SemaphoreType.DMA((len(units),)),
        ],
        compiler_params=pltpu.CompilerParams(vmem_limit_bytes=60 * 2**20),
        cost_estimate=pl.CostEstimate(flops=30 * 10**9, bytes_accessed=20 * 2**20, transcendentals=0),
    )(frames, taps, high, low)


def store_eight(y, left, b, depth, real, imag):
    rows, half, end = slice(128 * b, 128 * b + 128), depth + 128, depth + 256
    parts = [part.reshape(8 * TIME_BLOCKS, 128).astype(jnp.bfloat16) for part in (real, imag)]
    block = jnp.concatenate(parts, axis=0)
    turned = block.T
    y[depth:end, rows] = block
    left[0, rows, depth:end] = turned
    left[1, rows, depth:half] = turned[:, 128:]
    left[1, rows, half:end] = -turned[:, :128]


def store_four(y, left, b, depth, both):
    rows, end = slice(128 * b, 128 * b + 128), depth + 128
    swapped = jnp.concatenate([both[:, 4:], -both[:, :4]], axis=1)
    block, swapped = (
        part.reshape(8 * TIME_BLOCKS, 128).astype(jnp.bfloat16) for part in (both, swapped)
    )
    y[depth:end, rows] = block
    left[0, rows, depth:end] = block.T
    left[1, rows, depth:end] = swapped.T


def join_kernel(in_ref, y, left):
    for ch in range(DEVICE_CHANNELS):
        for b in range(ANTENNA_BLOCKS):
            sources, tile = pl.ds((b // 2) * TIME_BLOCKS, TIME_BLOCKS), b % 2

            def eight(row):
                return in_ref[sources, tile, row : row + 8, :].astype(jnp.float32)

            parts = []
            for part in range(2):
                tail = eight(32 + 16 * ch + 8 * part)
                none = jnp.zeros((1, 8, 128), jnp.float32)
                parts.append(eight(16 * ch + 8 * part) + jnp.concatenate([none, tail[:-1]], axis=0))
            store_eight(y.at[ch], left.at[ch], b, 0, *parts)
            store_four(y.at[ch], left.at[ch], b, 256, eight(64 + 8 * ch))


def join(received):
    vmem = pl.BlockSpec(memory_space=pltpu.VMEM)
    return pl.pallas_call(
        join_kernel,
        out_shape=(
            jax.ShapeDtypeStruct((DEVICE_CHANNELS, OLD_DEPTH, ANTENNA_COUNT), jnp.bfloat16),
            jax.ShapeDtypeStruct((DEVICE_CHANNELS, 2, ANTENNA_COUNT, OLD_DEPTH), jnp.bfloat16),
        ),
        in_specs=[vmem],
        out_specs=(vmem, vmem),
        compiler_params=pltpu.CompilerParams(vmem_limit_bytes=24 * 2**20),
        cost_estimate=pl.CostEstimate(flops=5 * 10**9, bytes_accessed=12 * 2**20, transcendentals=0),
    )(received)


def correlate_kernel(in_hbm, y_hbm, left_hbm, real_hbm, imag_hbm, *scratch):
    in_ref, y, left, tiles, in_sems, old_sems, out_sems = scratch

    def arriving(ch):
        tops = (0, 32, 64) if ch == 0 else (16, 48)
        return [
            pltpu.make_async_copy(
                in_hbm.at[:, :, pl.ds(top, 16)], in_ref.at[:, :, pl.ds(top, 16)], in_sems.at[top // 16]
            )
            for top in tops
        ]

    def arriving_old(ch):
        old = pl.ds(0, OLD_DEPTH)
        return (
            pltpu.make_async_copy(y_hbm.at[ch], y.at[ch, old], old_sems.at[ch, 0]),
            pltpu.make_async_copy(left_hbm.at[ch], left.at[ch, :, :, old], old_sems.at[ch, 1]),
        )

    for ch in range(DEVICE_CHANNELS):
        for copy in (*arriving(ch), *arriving_old(ch)):
            copy.start()
    dot = functools.partial(jnp.dot, preferred_element_type=jnp.float32)

    def first(i):
        return ANTENNA_BLOCKS * i - i * (i - 1) // 2

    def prepare(ch):
        for b in range(ANTENNA_BLOCKS):
            sources, tile = pl.ds((b // 2) * TIME_BLOCKS, TIME_BLOCKS), b % 2

            def eight(row):
                return in_ref[sources, tile, row : row + 8, :].astype(jnp.float32)

            for unit in range(2):
                row = 32 * unit + 16 * ch
                store_eight(y.at[ch], left.at[ch], b, OLD_DEPTH + 256 * unit, eight(row), eight(row + 8))
            store_four(y.at[ch], left.at[ch], b, OLD_DEPTH + 512, eight(64 + 8 * ch))

    def leaving(ch, pair):
        some = pl.ds(first(2 * pair), first(2 * pair + 2) - first(2 * pair))
        return [
            pltpu.make_async_copy(tiles.at[ch, part, some], ref.at[ch, some], out_sems.at[ch, pair, part])
            for part, ref in enumerate((real_hbm, imag_hbm))
        ]

    def multiply(ch):
        for pair in range(ANTENNA_BLOCKS // 2):
            rows = pl.ds(256 * pair, 256)
            lhs = left[ch, :, rows, :].reshape(512, DEPTH)
            for other in range(pair, ANTENNA_BLOCKS // 2):
                columns = pl.ds(256 * other, 256)
                found = dot(lhs, y[ch, :, columns]) * (1.0 / SPECTRA_COUNT)
                for a in range(2):
                    for b in range(2):
                        i, j = 2 * pair + a, 2 * other + b
                        if i <= j:
                            for part in range(2):
                                top = 256 * part + 128 * a
                                tiles[ch, part, first(i) + j - i] = found[
                                    top : top + 128, 128 * b : 128 * b + 128
                                ]
            for copy in leaving(ch, pair):
                copy.start()

    for ch in range(DEVICE_CHANNELS):
        for copy in arriving(ch):
            copy.wait()
        prepare(ch)
        for copy in arriving_old(ch):
            copy.wait()
        multiply(ch)
    for ch in range(DEVICE_CHANNELS):
        for pair in range(ANTENNA_BLOCKS // 2):
            for copy in leaving(ch, pair):
                copy.wait()


def correlate(received, y, left):
    out = jax.ShapeDtypeStruct((DEVICE_CHANNELS, PAIRS, 128, 128), jnp.float32)
    anywhere = pl.BlockSpec(memory_space=pl.ANY)
    return pl.pallas_call(
        correlate_kernel,
        out_shape=(out, out),
        in_specs=[anywhere] * 3,
        out_specs=(anywhere, anywhere),
        scratch_shapes=[
            pltpu.VMEM(received.shape, jnp.bfloat16),
            pltpu.VMEM((DEVICE_CHANNELS, DEPTH, ANTENNA_COUNT), jnp.bfloat16),
            pltpu.VMEM((DEVICE_CHANNELS, 2, ANTENNA_COUNT, DEPTH), jnp.bfloat16),
            pltpu.VMEM((DEVICE_CHANNELS, 2, PAIRS, 128, 128), jnp.float32),
            pltpu.SemaphoreType.DMA((5,)),
            pltpu.SemaphoreType.DMA((DEVICE_CHANNELS, 2)),
            pltpu.SemaphoreType.DMA((DEVICE_CHANNELS, ANTENNA_BLOCKS // 2, 2)),
        ],
        compiler_params=pltpu.CompilerParams(vmem_limit_bytes=60 * 2**20),
        cost_estimate=pl.CostEstimate(flops=5 * 10**9, bytes_accessed=12 * 2**20, transcendentals=0),
    )(received, y, left)


def exchange(departing):
    received = lax.all_to_all(departing, AXES, split_axis=0, concat_axis=0, tiled=True)
    return received.reshape(DEVICES // 2, 2, *received.shape[1:])


def on_device(voltages, taps):
    frames = voltages.reshape(TILE_ANTENNAS, FRAMES, 2, 8, 128).transpose(0, 1, 3, 2, 4)
    frames = frames.reshape(TILE_ANTENNAS, FRAMES, 16, 128)
    high, low = (jnp.asarray(table) for table in transform_tables())
    early = filterbank(frames, taps, high, low, EARLY_UNITS)
    taps, early = lax.optimization_barrier((taps, early))
    late = filterbank(frames, taps, high, low, LATE_UNITS)
    y, left = join(exchange(early))
    return correlate(exchange(late), y, left)


def solution(mesh):
    in_specs = (P(("grp", "tile"), "chan", None, None), P())
    out_specs = (P(AXES, None, None, None), P(AXES, None, None, None))
    return jax.shard_map(
        on_device, mesh=mesh, in_specs=in_specs, out_specs=out_specs, check_vma=False
    )
```

```python
import functools

import jax
import jax.numpy as jnp
import ml_dtypes
import numpy as np
from jax import lax
from jax.experimental import pallas as pl
from jax.experimental.pallas import tpu as pltpu
from jax.sharding import PartitionSpec as P

ANTENNA_COUNT = 1024
FRAME_SAMPLES = 1024
FILTER_TAPS = 8
ANTENNA_BLOCKS = 8
SPECTRA_COUNT = 512
DEVICE_CHANNELS = 2
TILE_ANTENNAS = 128
DEVICES = 128
FRAMES = 32
PIECE = 4
TIME_BLOCKS = 16
PAIRS = ANTENNA_BLOCKS * (ANTENNA_BLOCKS + 1) // 2
HALF = FRAME_SAMPLES // 2
AXES = ("grp", "chan", "tile")
SHARES = 4
SHARE = TILE_ANTENNAS // SHARES

EARLY_UNITS = ((0, 8), (32, 8), (8, 4))
LATE_UNITS = ((16, 8), (24, 8), (12, 4))
OLD_DEPTH = 2 * (8 + 4) * TIME_BLOCKS
DEPTH = 2 * FRAMES * TIME_BLOCKS


def transform_tables():
    sample = np.arange(HALF)
    parts = []
    for odd in range(2):
        channel = 2 * np.arange(DEVICES) + odd
        angle = 2.0 * np.pi * ((sample[:, None] * channel[None, :]) % FRAME_SAMPLES) / FRAME_SAMPLES
        cosine, sine = np.cos(angle), np.sin(angle)
        from_real = np.concatenate([cosine, -sine], axis=1)
        from_imag = np.concatenate([sine, cosine], axis=1)
        both = np.stack([from_real.reshape(4, 128, 256), from_imag.reshape(4, 128, 256)], axis=1)
        parts.append(both.reshape(FRAME_SAMPLES, 256))
    table = np.stack(parts).astype(np.float32)
    high = table.astype(ml_dtypes.bfloat16)
    low = (table - high.astype(np.float32)).astype(ml_dtypes.bfloat16)
    return high, low


def filterbank_kernel(units, order, x_hbm, taps_ref, high_hbm, low_hbm, out_hbm, *scratch):
    x_v, taps_rows, high_ref, low_ref, z, spectra, out_v, x_sems, table_sems, out_sems = scratch
    slot = {piece: i for i, piece in enumerate(order)}

    def arriving(i, share):
        antennas = pl.ds(SHARE * share, SHARE)
        return pltpu.make_async_copy(
            x_hbm.at[antennas, pl.ds(PIECE * order[i], PIECE)],
            x_v.at[antennas, pl.ds(PIECE * i, PIECE)],
            x_sems.at[i, share],
        )

    tables = [
        pltpu.make_async_copy(high_hbm, high_ref, table_sems.at[0]),
        pltpu.make_async_copy(low_hbm, low_ref, table_sems.at[1]),
    ]
    for share in range(SHARES):
        for i in range(2):
            arriving(i, share).start()
    for copy in tables:
        copy.start()
    for i in range(2, len(order)):
        for share in range(SHARES):
            arriving(i, share).start()
    for k in range(FILTER_TAPS):
        for j in range(8):
            row = taps_ref[k : k + 1, 128 * j : 128 * j + 128]
            taps_rows[k, 2 * j : 2 * j + 2, :] = jnp.broadcast_to(row, (2, 128))

    def inputs(start, count):
        return [s for s in range(start - FILTER_TAPS + 1, start + count) if 0 <= s < FRAMES]

    def filter_antenna(start, count, place, group, k8):
        a = group * 8 + k8
        frames = {
            s: x_v[a, slot[s // PIECE] * PIECE + s % PIECE].astype(jnp.float32)
            for s in inputs(start, count)
        }
        rows = pl.ds(pl.multiple_of(group * 64, 64) + k8, 8, stride=8)
        for q in range(count):
            total = None
            for k in range(FILTER_TAPS):
                s = start + q - k
                if s in frames:
                    term = taps_rows[k] * frames[s]
                    total = term if total is None else total + term
            if total is None:
                continue
            z[0, place + q, rows, :] = total[:8] + total[8:]
            z[1, place + q, rows, :] = total[:8] - total[8:]

    def transform(start, count, place, odd):
        top = 4 * place
        live = sum(1 for e in range(count) if inputs(start + e, 1))
        highs, lows = [], []
        for row in range(8):
            piece = jnp.concatenate(
                [
                    z[odd, place + e].reshape(TILE_ANTENNAS // 8, 8, 8, 128)[:, row].reshape(TILE_ANTENNAS, 128)
                    for e in range(live)
                ],
                axis=0,
            )
            high = piece.astype(jnp.bfloat16)
            highs.append(high)
            lows.append((piece - high.astype(jnp.float32)).astype(jnp.bfloat16))
        high = jnp.concatenate(highs, axis=1)
        low = jnp.concatenate(lows, axis=1)
        size = live * TILE_ANTENNAS
        dot = functools.partial(jnp.dot, preferred_element_type=jnp.float32)
        both = dot(jnp.concatenate([high, low], axis=0), high_ref[odd])
        found = (both[:size] + both[size:] + dot(high, low_ref[odd])).T
        step = 1024 if count == 8 else 4
        for part in range(2):
            for e in range(count):
                rows = pl.ds(step * part + e, DEVICES, stride=8)
                if e < live:
                    spectra[odd, rows, :] = found[128 * part : 128 * part + 128, 128 * e : 128 * e + 128]
                else:
                    spectra[odd, rows, :] = jnp.zeros((DEVICES, 128), jnp.float32)
        for n in range(count // 4):
            rows = spectra[odd, 1024 * n : 1024 * (n + 1), :].reshape(DEVICES, 8, 128)
            row = top + 2 * count * odd + 8 * n
            out_v[:, row : row + 8, :] = rows.astype(jnp.bfloat16)

    waited = 0
    place = 0
    leaving = []
    for u, (start, count) in enumerate(units):
        last = max(slot[s // PIECE] for s in inputs(start, count))

        def filter_step(group, _, start=start, count=count, place=place):
            for k8 in range(8):
                filter_antenna(start, count, place, group, k8)
            return 0

        def filter_share(share, _, last=last, waited=waited, filter_step=filter_step):
            for i in range(waited, last + 1):
                arriving(i, share).wait()
            lax.fori_loop(0, SHARE // 8, lambda n, c: filter_step(SHARE // 8 * share + n, c), 0)
            return 0

        if waited <= last:
            lax.fori_loop(0, SHARES, filter_share, 0)
            waited = last + 1
        else:
            lax.fori_loop(0, TILE_ANTENNAS // 8, filter_step, 0)
        place += count
    for copy in tables:
        copy.wait()
    place = 0
    for u, (start, count) in enumerate(units):
        for odd in range(2):
            transform(start, count, place, odd)
        rows = pl.ds(4 * place, 4 * count)
        copy = pltpu.make_async_copy(out_v.at[:, rows], out_hbm.at[:, rows], out_sems.at[u])
        copy.start()
        leaving.append(copy)
        place += count
    for copy in leaving:
        copy.wait()


def filterbank(frames, taps, high, low, units):
    order = []
    for start, count in units:
        for s in range(start - FILTER_TAPS + 1, start + count):
            if 0 <= s < FRAMES and s // PIECE not in order:
                order.append(s // PIECE)
    anywhere = pl.BlockSpec(memory_space=pl.ANY)
    shape = (DEVICES, 4 * sum(count for _, count in units), 128)
    table = pltpu.VMEM((2, FRAME_SAMPLES, 256), jnp.bfloat16)
    return pl.pallas_call(
        functools.partial(filterbank_kernel, units, tuple(order)),
        out_shape=jax.ShapeDtypeStruct(shape, jnp.bfloat16),
        in_specs=[anywhere, pl.BlockSpec(memory_space=pltpu.VMEM), anywhere, anywhere],
        out_specs=anywhere,
        scratch_shapes=[
            pltpu.VMEM((TILE_ANTENNAS, PIECE * len(order), 16, 128), jnp.bfloat16),
            pltpu.VMEM((FILTER_TAPS, 16, 128), jnp.float32),
            table,
            table,
            pltpu.VMEM((2, shape[1] // 4, 1024, 128), jnp.float32),
            pltpu.VMEM((2, 2048, 128), jnp.float32),
            pltpu.VMEM(shape, jnp.bfloat16),
            pltpu.SemaphoreType.DMA((len(order), SHARES)),
            pltpu.SemaphoreType.DMA((2,)),
            pltpu.SemaphoreType.DMA((len(units),)),
        ],
        compiler_params=pltpu.CompilerParams(vmem_limit_bytes=60 * 2**20),
        cost_estimate=pl.CostEstimate(flops=30 * 10**9, bytes_accessed=20 * 2**20, transcendentals=0),
    )(frames, taps, high, low)


def store_eight(y, left, b, depth, real, imag):
    rows, half, end = slice(128 * b, 128 * b + 128), depth + 128, depth + 256
    parts = [part.reshape(8 * TIME_BLOCKS, 128).astype(jnp.bfloat16) for part in (real, imag)]
    block = jnp.concatenate(parts, axis=0)
    turned = block.T
    y[depth:end, rows] = block
    left[0, rows, depth:end] = turned
    left[1, rows, depth:half] = turned[:, 128:]
    left[1, rows, half:end] = -turned[:, :128]


def store_four(y, left, b, depth, both):
    rows, end = slice(128 * b, 128 * b + 128), depth + 128
    swapped = jnp.concatenate([both[:, 4:], -both[:, :4]], axis=1)
    block, swapped = (
        part.reshape(8 * TIME_BLOCKS, 128).astype(jnp.bfloat16) for part in (both, swapped)
    )
    y[depth:end, rows] = block
    left[0, rows, depth:end] = block.T
    left[1, rows, depth:end] = swapped.T


def join_kernel(in_ref, y, left):
    for ch in range(DEVICE_CHANNELS):
        for b in range(ANTENNA_BLOCKS):
            sources, tile = pl.ds((b // 2) * TIME_BLOCKS, TIME_BLOCKS), b % 2

            def eight(row):
                return in_ref[sources, tile, row : row + 8, :].astype(jnp.float32)

            parts = []
            for part in range(2):
                tail = eight(32 + 16 * ch + 8 * part)
                none = jnp.zeros((1, 8, 128), jnp.float32)
                parts.append(eight(16 * ch + 8 * part) + jnp.concatenate([none, tail[:-1]], axis=0))
            store_eight(y.at[ch], left.at[ch], b, 0, *parts)
            store_four(y.at[ch], left.at[ch], b, 256, eight(64 + 8 * ch))


def join(received):
    vmem = pl.BlockSpec(memory_space=pltpu.VMEM)
    return pl.pallas_call(
        join_kernel,
        out_shape=(
            jax.ShapeDtypeStruct((DEVICE_CHANNELS, OLD_DEPTH, ANTENNA_COUNT), jnp.bfloat16),
            jax.ShapeDtypeStruct((DEVICE_CHANNELS, 2, ANTENNA_COUNT, OLD_DEPTH), jnp.bfloat16),
        ),
        in_specs=[vmem],
        out_specs=(vmem, vmem),
        compiler_params=pltpu.CompilerParams(vmem_limit_bytes=24 * 2**20),
        cost_estimate=pl.CostEstimate(flops=5 * 10**9, bytes_accessed=12 * 2**20, transcendentals=0),
    )(received)


def correlate_kernel(in_hbm, y_hbm, left_hbm, real_hbm, imag_hbm, *scratch):
    in_ref, y, left, tiles, in_sems, old_sems, out_sems = scratch

    def arriving(ch):
        tops = (0, 32, 64) if ch == 0 else (16, 48)
        return [
            pltpu.make_async_copy(
                in_hbm.at[:, :, pl.ds(top, 16)], in_ref.at[:, :, pl.ds(top, 16)], in_sems.at[top // 16]
            )
            for top in tops
        ]

    def arriving_old(ch):
        old = pl.ds(0, OLD_DEPTH)
        return (
            pltpu.make_async_copy(y_hbm.at[ch], y.at[ch, old], old_sems.at[ch, 0]),
            pltpu.make_async_copy(left_hbm.at[ch], left.at[ch, :, :, old], old_sems.at[ch, 1]),
        )

    for ch in range(DEVICE_CHANNELS):
        for copy in (*arriving(ch), *arriving_old(ch)):
            copy.start()
    dot = functools.partial(jnp.dot, preferred_element_type=jnp.float32)

    def first(i):
        return ANTENNA_BLOCKS * i - i * (i - 1) // 2

    def prepare(ch):
        for b in range(ANTENNA_BLOCKS):
            sources, tile = pl.ds((b // 2) * TIME_BLOCKS, TIME_BLOCKS), b % 2

            def eight(row):
                return in_ref[sources, tile, row : row + 8, :].astype(jnp.float32)

            for unit in range(2):
                row = 32 * unit + 16 * ch
                store_eight(y.at[ch], left.at[ch], b, OLD_DEPTH + 256 * unit, eight(row), eight(row + 8))
            store_four(y.at[ch], left.at[ch], b, OLD_DEPTH + 512, eight(64 + 8 * ch))

    def leaving(ch, pair):
        some = pl.ds(first(2 * pair), first(2 * pair + 2) - first(2 * pair))
        return [
            pltpu.make_async_copy(tiles.at[ch, part, some], ref.at[ch, some], out_sems.at[ch, pair, part])
            for part, ref in enumerate((real_hbm, imag_hbm))
        ]

    def multiply(ch):
        for pair in range(ANTENNA_BLOCKS // 2):
            rows = pl.ds(256 * pair, 256)
            lhs = left[ch, :, rows, :].reshape(512, DEPTH)
            for other in range(pair, ANTENNA_BLOCKS // 2):
                columns = pl.ds(256 * other, 256)
                found = dot(lhs, y[ch, :, columns]) * (1.0 / SPECTRA_COUNT)
                for a in range(2):
                    for b in range(2):
                        i, j = 2 * pair + a, 2 * other + b
                        if i <= j:
                            for part in range(2):
                                top = 256 * part + 128 * a
                                tiles[ch, part, first(i) + j - i] = found[
                                    top : top + 128, 128 * b : 128 * b + 128
                                ]
            for copy in leaving(ch, pair):
                copy.start()

    for ch in range(DEVICE_CHANNELS):
        for copy in arriving(ch):
            copy.wait()
        prepare(ch)
        for copy in arriving_old(ch):
            copy.wait()
        multiply(ch)
    for ch in range(DEVICE_CHANNELS):
        for pair in range(ANTENNA_BLOCKS // 2):
            for copy in leaving(ch, pair):
                copy.wait()


def correlate(received, y, left):
    out = jax.ShapeDtypeStruct((DEVICE_CHANNELS, PAIRS, 128, 128), jnp.float32)
    anywhere = pl.BlockSpec(memory_space=pl.ANY)
    return pl.pallas_call(
        correlate_kernel,
        out_shape=(out, out),
        in_specs=[anywhere] * 3,
        out_specs=(anywhere, anywhere),
        scratch_shapes=[
            pltpu.VMEM(received.shape, jnp.bfloat16),
            pltpu.VMEM((DEVICE_CHANNELS, DEPTH, ANTENNA_COUNT), jnp.bfloat16),
            pltpu.VMEM((DEVICE_CHANNELS, 2, ANTENNA_COUNT, DEPTH), jnp.bfloat16),
            pltpu.VMEM((DEVICE_CHANNELS, 2, PAIRS, 128, 128), jnp.float32),
            pltpu.SemaphoreType.DMA((5,)),
            pltpu.SemaphoreType.DMA((DEVICE_CHANNELS, 2)),
            pltpu.SemaphoreType.DMA((DEVICE_CHANNELS, ANTENNA_BLOCKS // 2, 2)),
        ],
        compiler_params=pltpu.CompilerParams(vmem_limit_bytes=60 * 2**20),
        cost_estimate=pl.CostEstimate(flops=5 * 10**9, bytes_accessed=12 * 2**20, transcendentals=0),
    )(received, y, left)


def exchange(departing):
    received = lax.all_to_all(departing, AXES, split_axis=0, concat_axis=0, tiled=True)
    return received.reshape(DEVICES // 2, 2, *received.shape[1:])


def on_device(voltages, taps):
    frames = voltages.reshape(TILE_ANTENNAS, FRAMES, 2, 8, 128).transpose(0, 1, 3, 2, 4)
    frames = frames.reshape(TILE_ANTENNAS, FRAMES, 16, 128)
    high, low = (jnp.asarray(table) for table in transform_tables())
    early = filterbank(frames, taps, high, low, EARLY_UNITS)
    taps, early = lax.optimization_barrier((taps, early))
    late = filterbank(frames, taps, high, low, LATE_UNITS)
    y, left = join(exchange(early))
    return correlate(exchange(late), y, left)


def solution(mesh):
    in_specs = (P(("grp", "tile"), "chan", None, None), P())
    out_specs = (P(AXES, None, None, None), P(AXES, None, None, None))
    return jax.shard_map(
        on_device, mesh=mesh, in_specs=in_specs, out_specs=out_specs, check_vma=False
    )
```

```python
import functools

import jax
import jax.numpy as jnp
import ml_dtypes
import numpy as np
from jax import lax
from jax.experimental import pallas as pl
from jax.experimental.pallas import tpu as pltpu
from jax.sharding import PartitionSpec as P

ANTENNA_COUNT = 1024
FRAME_SAMPLES = 1024
FILTER_TAPS = 8
ANTENNA_BLOCKS = 8
SPECTRA_COUNT = 512
DEVICE_CHANNELS = 2
TILE_ANTENNAS = 128
DEVICES = 128
FRAMES = 32
PIECE = 4
TIME_BLOCKS = 16
PAIRS = ANTENNA_BLOCKS * (ANTENNA_BLOCKS + 1) // 2
HALF = FRAME_SAMPLES // 2
AXES = ("grp", "chan", "tile")
SHARES = 4
SHARE = TILE_ANTENNAS // SHARES

EARLY_UNITS = ((0, 8), (32, 8), (8, 4))
LATE_UNITS = ((16, 8), (24, 8), (12, 4))
OLD_DEPTH = 2 * (8 + 4) * TIME_BLOCKS
DEPTH = 2 * FRAMES * TIME_BLOCKS


def transform_tables():
    sample = np.arange(HALF)
    parts = []
    for odd in range(2):
        channel = 2 * np.arange(DEVICES) + odd
        angle = 2.0 * np.pi * ((sample[:, None] * channel[None, :]) % FRAME_SAMPLES) / FRAME_SAMPLES
        cosine, sine = np.cos(angle), np.sin(angle)
        from_real = np.concatenate([cosine, -sine], axis=1)
        from_imag = np.concatenate([sine, cosine], axis=1)
        both = np.stack([from_real.reshape(4, 128, 256), from_imag.reshape(4, 128, 256)], axis=1)
        parts.append(both.reshape(FRAME_SAMPLES, 256))
    table = np.stack(parts).astype(np.float32)
    high = table.astype(ml_dtypes.bfloat16)
    low = (table - high.astype(np.float32)).astype(ml_dtypes.bfloat16)
    return high, low


def filterbank_kernel(units, order, x_hbm, taps_ref, high_hbm, low_hbm, out_hbm, *scratch):
    x_v, taps_rows, high_ref, low_ref, z, spectra, out_v, x_sems, table_sems, out_sems = scratch
    slot = {piece: i for i, piece in enumerate(order)}

    def arriving(i, share):
        antennas = pl.ds(SHARE * share, SHARE)
        return pltpu.make_async_copy(
            x_hbm.at[antennas, pl.ds(PIECE * order[i], PIECE)],
            x_v.at[antennas, pl.ds(PIECE * i, PIECE)],
            x_sems.at[i, share],
        )

    tables = [
        pltpu.make_async_copy(high_hbm, high_ref, table_sems.at[0]),
        pltpu.make_async_copy(low_hbm, low_ref, table_sems.at[1]),
    ]
    for share in range(SHARES):
        for i in range(2):
            arriving(i, share).start()
    for copy in tables:
        copy.start()
    for i in range(2, len(order)):
        for share in range(SHARES):
            arriving(i, share).start()
    for k in range(FILTER_TAPS):
        for j in range(8):
            row = taps_ref[k : k + 1, 128 * j : 128 * j + 128]
            taps_rows[k, 2 * j : 2 * j + 2, :] = jnp.broadcast_to(row, (2, 128))

    def inputs(start, count):
        return [s for s in range(start - FILTER_TAPS + 1, start + count) if 0 <= s < FRAMES]

    def filter_antenna(start, count, place, group, k8):
        a = group * 8 + k8
        frames = {
            s: x_v[a, slot[s // PIECE] * PIECE + s % PIECE].astype(jnp.float32)
            for s in inputs(start, count)
        }
        rows = pl.ds(pl.multiple_of(group * 64, 64) + k8, 8, stride=8)
        for q in range(count):
            total = None
            for k in range(FILTER_TAPS):
                s = start + q - k
                if s in frames:
                    term = taps_rows[k] * frames[s]
                    total = term if total is None else total + term
            if total is None:
                continue
            z[0, place + q, rows, :] = total[:8] + total[8:]
            z[1, place + q, rows, :] = total[:8] - total[8:]

    def transform(start, count, place, odd):
        top = 4 * place
        live = sum(1 for e in range(count) if inputs(start + e, 1))
        highs, lows = [], []
        for row in range(8):
            piece = jnp.concatenate(
                [
                    z[odd, place + e].reshape(TILE_ANTENNAS // 8, 8, 8, 128)[:, row].reshape(TILE_ANTENNAS, 128)
                    for e in range(live)
                ],
                axis=0,
            )
            high = piece.astype(jnp.bfloat16)
            highs.append(high)
            lows.append((piece - high.astype(jnp.float32)).astype(jnp.bfloat16))
        high = jnp.concatenate(highs, axis=1)
        low = jnp.concatenate(lows, axis=1)
        size = live * TILE_ANTENNAS
        dot = functools.partial(jnp.dot, preferred_element_type=jnp.float32)
        both = dot(jnp.concatenate([high, low], axis=0), high_ref[odd])
        found = (both[:size] + both[size:] + dot(high, low_ref[odd])).T
        step = 1024 if count == 8 else 4
        for part in range(2):
            for e in range(count):
                rows = pl.ds(step * part + e, DEVICES, stride=8)
                if e < live:
                    spectra[odd, rows, :] = found[128 * part : 128 * part + 128, 128 * e : 128 * e + 128]
                else:
                    spectra[odd, rows, :] = jnp.zeros((DEVICES, 128), jnp.float32)
        for n in range(count // 4):
            rows = spectra[odd, 1024 * n : 1024 * (n + 1), :].reshape(DEVICES, 8, 128)
            row = top + 2 * count * odd + 8 * n
            out_v[:, row : row + 8, :] = rows.astype(jnp.bfloat16)

    waited = 0
    place = 0
    leaving = []
    for u, (start, count) in enumerate(units):
        last = max(slot[s // PIECE] for s in inputs(start, count))

        def filter_step(group, _, start=start, count=count, place=place):
            for k8 in range(8):
                filter_antenna(start, count, place, group, k8)
            return 0

        def filter_share(share, _, last=last, waited=waited, filter_step=filter_step):
            for i in range(waited, last + 1):
                arriving(i, share).wait()
            lax.fori_loop(0, SHARE // 8, lambda n, c: filter_step(SHARE // 8 * share + n, c), 0)
            return 0

        if waited <= last:
            lax.fori_loop(0, SHARES, filter_share, 0)
            waited = last + 1
        else:
            lax.fori_loop(0, TILE_ANTENNAS // 8, filter_step, 0)
        place += count
    for copy in tables:
        copy.wait()
    place = 0
    for u, (start, count) in enumerate(units):
        for odd in range(2):
            transform(start, count, place, odd)
        rows = pl.ds(4 * place, 4 * count)
        copy = pltpu.make_async_copy(out_v.at[:, rows], out_hbm.at[:, rows], out_sems.at[u])
        copy.start()
        leaving.append(copy)
        place += count
    for copy in leaving:
        copy.wait()


def filterbank(frames, taps, high, low, units):
    order = []
    for start, count in units:
        for s in range(start - FILTER_TAPS + 1, start + count):
            if 0 <= s < FRAMES and s // PIECE not in order:
                order.append(s // PIECE)
    anywhere = pl.BlockSpec(memory_space=pl.ANY)
    shape = (DEVICES, 4 * sum(count for _, count in units), 128)
    table = pltpu.VMEM((2, FRAME_SAMPLES, 256), jnp.bfloat16)
    return pl.pallas_call(
        functools.partial(filterbank_kernel, units, tuple(order)),
        out_shape=jax.ShapeDtypeStruct(shape, jnp.bfloat16),
        in_specs=[anywhere, pl.BlockSpec(memory_space=pltpu.VMEM), anywhere, anywhere],
        out_specs=anywhere,
        scratch_shapes=[
            pltpu.VMEM((TILE_ANTENNAS, PIECE * len(order), 16, 128), jnp.bfloat16),
            pltpu.VMEM((FILTER_TAPS, 16, 128), jnp.float32),
            table,
            table,
            pltpu.VMEM((2, shape[1] // 4, 1024, 128), jnp.float32),
            pltpu.VMEM((2, 2048, 128), jnp.float32),
            pltpu.VMEM(shape, jnp.bfloat16),
            pltpu.SemaphoreType.DMA((len(order), SHARES)),
            pltpu.SemaphoreType.DMA((2,)),
            pltpu.SemaphoreType.DMA((len(units),)),
        ],
        compiler_params=pltpu.CompilerParams(vmem_limit_bytes=60 * 2**20),
        cost_estimate=pl.CostEstimate(flops=30 * 10**9, bytes_accessed=20 * 2**20, transcendentals=0),
    )(frames, taps, high, low)


def store_eight(y, left, b, depth, real, imag):
    rows, half, end = slice(128 * b, 128 * b + 128), depth + 128, depth + 256
    parts = [part.reshape(8 * TIME_BLOCKS, 128).astype(jnp.bfloat16) for part in (real, imag)]
    block = jnp.concatenate(parts, axis=0)
    turned = block.T
    y[depth:end, rows] = block
    left[0, rows, depth:end] = turned
    left[1, rows, depth:half] = turned[:, 128:]
    left[1, rows, half:end] = -turned[:, :128]


def store_four(y, left, b, depth, both):
    rows, end = slice(128 * b, 128 * b + 128), depth + 128
    swapped = jnp.concatenate([both[:, 4:], -both[:, :4]], axis=1)
    block, swapped = (
        part.reshape(8 * TIME_BLOCKS, 128).astype(jnp.bfloat16) for part in (both, swapped)
    )
    y[depth:end, rows] = block
    left[0, rows, depth:end] = block.T
    left[1, rows, depth:end] = swapped.T


def join_kernel(in_ref, y, left):
    for ch in range(DEVICE_CHANNELS):
        for b in range(ANTENNA_BLOCKS):
            sources, tile = pl.ds((b // 2) * TIME_BLOCKS, TIME_BLOCKS), b % 2

            def eight(row):
                return in_ref[sources, tile, row : row + 8, :].astype(jnp.float32)

            parts = []
            for part in range(2):
                tail = eight(32 + 16 * ch + 8 * part)
                none = jnp.zeros((1, 8, 128), jnp.float32)
                parts.append(eight(16 * ch + 8 * part) + jnp.concatenate([none, tail[:-1]], axis=0))
            store_eight(y.at[ch], left.at[ch], b, 0, *parts)
            store_four(y.at[ch], left.at[ch], b, 256, eight(64 + 8 * ch))


def join(received):
    vmem = pl.BlockSpec(memory_space=pltpu.VMEM)
    return pl.pallas_call(
        join_kernel,
        out_shape=(
            jax.ShapeDtypeStruct((DEVICE_CHANNELS, OLD_DEPTH, ANTENNA_COUNT), jnp.bfloat16),
            jax.ShapeDtypeStruct((DEVICE_CHANNELS, 2, ANTENNA_COUNT, OLD_DEPTH), jnp.bfloat16),
        ),
        in_specs=[vmem],
        out_specs=(vmem, vmem),
        compiler_params=pltpu.CompilerParams(vmem_limit_bytes=24 * 2**20),
        cost_estimate=pl.CostEstimate(flops=5 * 10**9, bytes_accessed=12 * 2**20, transcendentals=0),
    )(received)


def correlate_kernel(in_hbm, y_hbm, left_hbm, real_hbm, imag_hbm, *scratch):
    in_ref, y, left, tiles, in_sems, old_sems, out_sems = scratch

    def arriving(ch):
        tops = (0, 32, 64) if ch == 0 else (16, 48)
        return [
            pltpu.make_async_copy(
                in_hbm.at[:, :, pl.ds(top, 16)], in_ref.at[:, :, pl.ds(top, 16)], in_sems.at[top // 16]
            )
            for top in tops
        ]

    def arriving_old(ch):
        old = pl.ds(0, OLD_DEPTH)
        return (
            pltpu.make_async_copy(y_hbm.at[ch], y.at[ch, old], old_sems.at[ch, 0]),
            pltpu.make_async_copy(left_hbm.at[ch, 0], left.at[ch, 0, :, old], old_sems.at[ch, 1]),
            pltpu.make_async_copy(
                left_hbm.at[ch, 1, :, pl.ds(256, 128)], left.at[ch, 1, :, pl.ds(256, 128)], old_sems.at[ch, 2]
            ),
        )

    for ch in range(DEVICE_CHANNELS):
        for copy in (*arriving(ch), *arriving_old(ch)):
            copy.start()
    dot = functools.partial(jnp.dot, preferred_element_type=jnp.float32)

    def first(i):
        return ANTENNA_BLOCKS * i - i * (i - 1) // 2

    def prepare(ch):
        for b in range(ANTENNA_BLOCKS):
            sources, tile = pl.ds((b // 2) * TIME_BLOCKS, TIME_BLOCKS), b % 2

            def eight(row):
                return in_ref[sources, tile, row : row + 8, :].astype(jnp.float32)

            for unit in range(2):
                row = 32 * unit + 16 * ch
                store_eight(y.at[ch], left.at[ch], b, OLD_DEPTH + 256 * unit, eight(row), eight(row + 8))
            store_four(y.at[ch], left.at[ch], b, OLD_DEPTH + 512, eight(64 + 8 * ch))

    def leaving(ch, pair):
        some = pl.ds(first(2 * pair), first(2 * pair + 2) - first(2 * pair))
        return [
            pltpu.make_async_copy(tiles.at[ch, part, some], ref.at[ch, some], out_sems.at[ch, pair, part])
            for part, ref in enumerate((real_hbm, imag_hbm))
        ]

    def multiply(ch):
        for pair in range(ANTENNA_BLOCKS // 2):
            rows = pl.ds(256 * pair, 256)
            lhs = left[ch, :, rows, :].reshape(512, DEPTH)
            for other in range(pair, ANTENNA_BLOCKS // 2):
                columns = pl.ds(256 * other, 256)
                found = dot(lhs, y[ch, :, columns]) * (1.0 / SPECTRA_COUNT)
                for a in range(2):
                    for b in range(2):
                        i, j = 2 * pair + a, 2 * other + b
                        if i <= j:
                            for part in range(2):
                                top = 256 * part + 128 * a
                                tiles[ch, part, first(i) + j - i] = found[
                                    top : top + 128, 128 * b : 128 * b + 128
                                ]
            for copy in leaving(ch, pair):
                copy.start()

    for ch in range(DEVICE_CHANNELS):
        for copy in arriving(ch):
            copy.wait()
        prepare(ch)
        for copy in arriving_old(ch):
            copy.wait()
        left[ch, 1, :, 0:128] = left[ch, 0, :, 128:256]
        left[ch, 1, :, 128:256] = -left[ch, 0, :, 0:128]
        multiply(ch)
    for ch in range(DEVICE_CHANNELS):
        for pair in range(ANTENNA_BLOCKS // 2):
            for copy in leaving(ch, pair):
                copy.wait()


def correlate(received, y, left):
    out = jax.ShapeDtypeStruct((DEVICE_CHANNELS, PAIRS, 128, 128), jnp.float32)
    anywhere = pl.BlockSpec(memory_space=pl.ANY)
    return pl.pallas_call(
        correlate_kernel,
        out_shape=(out, out),
        in_specs=[anywhere] * 3,
        out_specs=(anywhere, anywhere),
        scratch_shapes=[
            pltpu.VMEM(received.shape, jnp.bfloat16),
            pltpu.VMEM((DEVICE_CHANNELS, DEPTH, ANTENNA_COUNT), jnp.bfloat16),
            pltpu.VMEM((DEVICE_CHANNELS, 2, ANTENNA_COUNT, DEPTH), jnp.bfloat16),
            pltpu.VMEM((DEVICE_CHANNELS, 2, PAIRS, 128, 128), jnp.float32),
            pltpu.SemaphoreType.DMA((5,)),
            pltpu.SemaphoreType.DMA((DEVICE_CHANNELS, 3)),
            pltpu.SemaphoreType.DMA((DEVICE_CHANNELS, ANTENNA_BLOCKS // 2, 2)),
        ],
        compiler_params=pltpu.CompilerParams(vmem_limit_bytes=60 * 2**20),
        cost_estimate=pl.CostEstimate(flops=5 * 10**9, bytes_accessed=12 * 2**20, transcendentals=0),
    )(received, y, left)


def exchange(departing):
    received = lax.all_to_all(departing, AXES, split_axis=0, concat_axis=0, tiled=True)
    return received.reshape(DEVICES // 2, 2, *received.shape[1:])


def on_device(voltages, taps):
    frames = voltages.reshape(TILE_ANTENNAS, FRAMES, 2, 8, 128).transpose(0, 1, 3, 2, 4)
    frames = frames.reshape(TILE_ANTENNAS, FRAMES, 16, 128)
    high, low = (jnp.asarray(table) for table in transform_tables())
    early = filterbank(frames, taps, high, low, EARLY_UNITS)
    taps, early = lax.optimization_barrier((taps, early))
    late = filterbank(frames, taps, high, low, LATE_UNITS)
    y, left = join(exchange(early))
    return correlate(exchange(late), y, left)


def solution(mesh):
    in_specs = (P(("grp", "tile"), "chan", None, None), P())
    out_specs = (P(AXES, None, None, None), P(AXES, None, None, None))
    return jax.shard_map(
        on_device, mesh=mesh, in_specs=in_specs, out_specs=out_specs, check_vma=False
    )
```
